256 devices in a mesh: dp: 32 (over y, x, core), chain: 8 (over z).
Axes of the slice: x: 4, y: 4, z: 8, core: 2. Of those that a mesh axis runs over, the one named last changes fastest.
Arguments:
- events: bfloat16 [32, 1024, 1024], P('dp', 'chain'), may hold values from -6 to 6
- destinations: int32 [32, 1024], P('dp', 'chain'), may hold values from 0 to 4095, as said below
- history_ids: int32 [32, 1024], P('dp'), may hold values from 0 to 2, never falling along the last dimension, each value on 1 to 768 neighbouring positions
- cotangent: bfloat16 [32, 1024, 1024], P('dp', 'chain'), may hold values from -6 to 6
- w_uvqk: bfloat16 [1024, 4096], replicated, may hold values from -0.1875 to 0.1875
- w_out: bfloat16 [1024, 1024], replicated, may hold values from -0.1875 to 0.1875
Outputs:
- layer_out: bfloat16 [32, 1024, 1024], P('dp', 'chain')
- event_grad: bfloat16 [32, 1024, 1024], P('dp', 'chain')
- weight_grad: float32 [1024, 1024], P('dp')
The draws below stay inside these ranges and needn't reach their ends.
Inputs may be any that keep to these rules, and one draw needn't show every extreme that they name: destinations[d, c * 128 + i] = e * 128 + s moves that event to row c * 128 + s of group e; the map is one to one, and every device sends an equal share of its events to each dp index. history_ids never fall along a group; in each group one history holds exactly 768 events and the other histories share the rest.
All inputs are finite; a program needn't handle non-finite values.
Results may differ from the reference program's by a relative error of at most 0.025.
Values may be sent and summed in bfloat16 or wider, within the bound.
A program may use at most 128 MiB of HBM per device.

```python
import math
import jax
import jax.numpy as jnp
import numpy as np
from jax import lax

D = 1024
HEADS = 8
ROWS = 128
HISTS = 3
TOKG = 1024
TOKENS = 32768
N_DP = 32
N_CHAIN = 8


def draw_destinations(key, part):
    key = jax.random.fold_in(key, 7)
    send_key, slot_key = jax.random.split(key)
    per_peer = ROWS // N_DP
    device_total = N_DP * N_CHAIN
    send_order = jax.vmap(lambda subkey: jax.random.permutation(subkey, ROWS))(jax.random.split(send_key, device_total))
    slot_order = jax.vmap(lambda subkey: jax.random.permutation(subkey, ROWS))(jax.random.split(slot_key, device_total))
    send_order = send_order.reshape(N_DP, N_CHAIN, ROWS).astype(jnp.int32)
    slot_order = slot_order.reshape(N_DP, N_CHAIN, ROWS).astype(jnp.int32)
    target = send_order // per_peer
    within = send_order % per_peer
    sender = jnp.arange(N_DP, dtype=jnp.int32)[:, None, None]
    column = jnp.broadcast_to(jnp.arange(N_CHAIN, dtype=jnp.int32)[None, :, None], target.shape)
    slot_index = slot_order[target, column, sender * per_peer + within]
    return (target * ROWS + slot_index).reshape(N_DP, N_CHAIN * ROWS).astype(jnp.int32)


def level_of(own_key, shape, cuts, smallest, high):
    gain = 1.0
    for dim, blocks in cuts:
        steps = jax.random.uniform(jax.random.fold_in(jax.random.fold_in(own_key, 6), dim), (blocks,), jnp.float32, smallest / len(cuts), high / len(cuts))
        gain = gain * jnp.repeat(jnp.exp(steps), shape[dim] // blocks).reshape((-1,) + (1,) * (len(shape) - 1 - dim))
    return gain


def length_profile(number_of, total, limit, lean):
    portions = [(1 << 20) // math.isqrt(standing ** lean) + 1 for standing in range(2, number_of + 1)]
    rest, given = total - limit - (number_of - 1), [1] * (number_of - 1)
    while rest > 0:
        movable = [i for i in range(number_of - 1) if given[i] < limit]
        pool, remaining = sum([portions[i] for i in movable]), rest
        for i in movable:
            extra = min(limit - given[i], max(1, remaining * portions[i] // pool), rest)
            given[i] = given[i] + extra
            rest = rest - extra
    return np.array([limit] + given)


def uneven(own_key, number_of, total, reach, slope):
    if number_of == 2:
        one = jax.random.randint(own_key, (), max(1, total - reach), min(reach, total - 1) + 1)
        return jnp.stack([one, total - one])
    sizes = jnp.asarray(length_profile(number_of, total, reach, slope), jnp.int32)
    twos = (number_of - 1) // 2
    source_of, taker = sizes[1:1 + 2 * twos:2], sizes[2:2 + 2 * twos:2]
    margin = jnp.minimum(source_of - 1, reach - taker)
    passed = jax.random.randint(jax.random.fold_in(own_key, 1), (twos,), 0, 1 << 20) % (margin + 1)
    sizes = sizes.at[1:1 + 2 * twos:2].set(source_of - passed).at[2:2 + 2 * twos:2].set(taker + passed)
    return sizes[jax.random.permutation(jax.random.fold_in(own_key, 2), number_of)]


def centred(key, dims, deviation, limit, pieces=(), held_as=jnp.bfloat16):
    array = jax.random.normal(key, dims, jnp.float32) * deviation
    if len(pieces) > 0:
        array = level_of(key, dims, pieces, -0.22, 0.18) * array
    return jnp.clip(array, min=-limit, max=limit).astype(held_as)


def setup_inputs(seed: int = 0) -> dict:
    keys = jax.random.split(jax.random.key(seed), 7)
    return {
        "events": centred(keys[0], (N_DP, TOKG, D), 1.0, 6.0, ((0, 32), (1, 8))),
        "destinations": draw_destinations(jax.random.fold_in(keys[6], 71), 0),
        "history_ids": jax.vmap(lambda own: jnp.searchsorted(jnp.cumsum(uneven(own, HISTS, TOKG, 3 * TOKG // 4, 0)), jnp.arange(TOKG), side="right"))(jax.random.split(keys[2], N_DP)).reshape((N_DP, TOKG)).astype(jnp.int32),
        "cotangent": centred(keys[3], (N_DP, TOKG, D), 1.0, 6.0, ((0, 32), (1, 8))),
        "w_uvqk": centred(keys[4], (D, 4 * D), D ** -0.5, 0.1875),
        "w_out": centred(keys[5], (D, D), D ** -0.5, 0.1875),
    }


epsilon = 1e-05

def layer_norm(values):
    center = values - lax.optimization_barrier(jnp.mean(values, axis=-1, keepdims=True))
    variance = lax.optimization_barrier(jnp.mean(center * center, axis=-1, keepdims=True))
    return center * lax.rsqrt(variance + epsilon)

def norm_back(values, upstream):
    center = values - lax.optimization_barrier(jnp.mean(values, axis=-1, keepdims=True))
    variance = lax.optimization_barrier(jnp.mean(center * center, axis=-1, keepdims=True))
    inverse = lax.rsqrt(variance + epsilon)
    normed = center * inverse
    upstream_mean = lax.optimization_barrier(jnp.mean(upstream, axis=-1, keepdims=True))
    product_mean = lax.optimization_barrier(jnp.mean(upstream * normed, axis=-1, keepdims=True))
    return inverse * (upstream - upstream_mean - normed * product_mean)

def silu_slope(values):
    sigmoid = jax.nn.sigmoid(values)
    return sigmoid * (1.0 + values * (1.0 - sigmoid))

def one_group(inputs, w_uvqk, w_out):
    grouped, history, upstream = inputs
    token_total = grouped.shape[0]
    model_width = grouped.shape[1]
    head_dim = model_width // HEADS
    alpha = head_dim ** (-0.5)
    residual = grouped.astype(jnp.float32)
    normed = layer_norm(residual).astype(jnp.bfloat16)
    pre_act = jnp.dot(normed, w_uvqk, preferred_element_type=jnp.float32)
    projected = jax.nn.silu(pre_act).astype(jnp.bfloat16).astype(jnp.float32)
    gating = projected[:, :model_width]
    values_all = projected[:, model_width:2 * model_width].reshape(token_total, HEADS, head_dim)
    queries = projected[:, 2 * model_width:3 * model_width].reshape(token_total, HEADS, head_dim)
    keys_all = projected[:, 3 * model_width:].reshape(token_total, HEADS, head_dim)
    position = jnp.arange(token_total, dtype=jnp.int32)
    visible = (history[:, None] == history[None, :]) & (position[None, :] <= position[:, None])
    scores = jnp.einsum('qhd,khd->hqk', queries, keys_all) * alpha
    attention = jnp.where(visible[None], jax.nn.silu(scores), 0.0).astype(jnp.bfloat16)
    attention_wide = attention.astype(jnp.float32)
    mixed = jnp.einsum('hqk,khd->qhd', attention_wide, values_all).reshape(token_total, model_width)
    mixed_norm = layer_norm(mixed)
    gated = (mixed_norm * gating).astype(jnp.bfloat16)
    layer_out = (residual + jnp.dot(gated, w_out, preferred_element_type=jnp.float32)).astype(jnp.bfloat16)
    gated_grad = jnp.dot(upstream, w_out.T, preferred_element_type=jnp.float32)
    gating_grad = gated_grad * mixed_norm
    mixed_grad = norm_back(mixed, gated_grad * gating).astype(jnp.bfloat16)
    mixed_heads = mixed_grad.astype(jnp.float32).reshape(token_total, HEADS, head_dim)
    attention_grad = jnp.einsum('qhd,khd->hqk', mixed_heads, values_all)
    score_grad = jnp.where(visible[None], attention_grad * silu_slope(scores) * alpha, 0.0).astype(jnp.bfloat16)
    score_wide = score_grad.astype(jnp.float32)
    query_grad = jnp.einsum('hqk,khd->qhd', score_wide, keys_all).reshape(token_total, model_width)
    blocks = token_total // ROWS
    score_split = score_wide.reshape(HEADS, blocks, ROWS, token_total)
    attention_split = attention_wide.reshape(HEADS, blocks, ROWS, token_total)
    query_split = queries.reshape(blocks, ROWS, HEADS, head_dim)
    mixed_split = mixed_heads.reshape(blocks, ROWS, HEADS, head_dim)
    key_terms = jnp.einsum('hcqk,cqhd->ckhd', score_split, query_split)
    value_terms = jnp.einsum('hcqk,cqhd->ckhd', attention_split, mixed_split)
    key_terms = lax.optimization_barrier(key_terms.astype(jnp.bfloat16)).astype(jnp.float32)
    value_terms = lax.optimization_barrier(value_terms.astype(jnp.bfloat16)).astype(jnp.float32)
    key_grad = lax.optimization_barrier(jnp.sum(key_terms, axis=0)).reshape(token_total, model_width)
    value_grad = lax.optimization_barrier(jnp.sum(value_terms, axis=0)).reshape(token_total, model_width)
    pre_grad = (jnp.concatenate([gating_grad, value_grad, query_grad, key_grad], axis=1) * silu_slope(pre_act)).astype(jnp.bfloat16)
    normed_grad = jnp.dot(pre_grad, w_uvqk.T, preferred_element_type=jnp.float32)
    input_grad = (upstream.astype(jnp.float32) + norm_back(residual, normed_grad)).astype(jnp.bfloat16)
    weight_term = jnp.dot(gated.T, upstream, preferred_element_type=jnp.float32) * (1.0 / math.sqrt(TOKENS))
    return (layer_out, input_grad, weight_term)

def reference(events, destinations, history_ids, cotangent, w_uvqk, w_out):
    group_count = events.shape[0]
    token_total = events.shape[1]
    model_width = events.shape[2]
    column = (jnp.arange(token_total, dtype=jnp.int32) // ROWS).astype(jnp.int32)
    flat_index = (destinations // ROWS * token_total + column[None, :] * ROWS + destinations % ROWS).reshape(-1).astype(jnp.int32)
    flat_events = events.reshape(group_count * token_total, model_width)
    grouped = jnp.zeros_like(flat_events).at[flat_index].set(flat_events).reshape(events.shape)

    def step_group(total, inputs):
        layer_out, input_grad, weight_term = one_group(inputs, w_uvqk, w_out)
        return (total + weight_term, (layer_out, input_grad))
    start_total = jnp.zeros((model_width, model_width), jnp.float32)
    weight_grad, outputs = lax.scan(step_group, start_total, (grouped, history_ids, cotangent))
    layer_out, grouped_grad = outputs
    event_grad = grouped_grad.reshape(group_count * token_total, model_width)[flat_index].reshape(events.shape)
    return (layer_out, event_grad, weight_grad)
```

```python
import functools
import math

import jax
import jax.numpy as jnp
from jax import lax
from jax.experimental import pallas as pl
from jax.experimental.pallas import tpu as pltpu
from jax.sharding import PartitionSpec as P

HEADS = 8
MESH = pl.DeviceIdType.MESH
BF = jnp.bfloat16
F32 = jnp.float32
I32 = jnp.int32
epsilon = 1e-05


def dot(a, b):
    return lax.dot_general(a, b, (((1,), (0,)), ((), ())), preferred_element_type=F32)


def dot_nt(a, b):
    return lax.dot_general(a, b, (((1,), (1,)), ((), ())), preferred_element_type=F32)


def dot_tn(a, b):
    return lax.dot_general(a, b, (((0,), (0,)), ((), ())), preferred_element_type=F32)


def sigmoid(v):
    return 0.5 * jnp.tanh(0.5 * v) + 0.5


def iota(shape, dim):
    return lax.broadcasted_iota(I32, shape, dim)


def mean(v):
    return jnp.mean(v, axis=-1, keepdims=True)


def one_hot(mask):
    return jnp.where(mask, 1.0, 0.0).astype(BF)


def kernel(
    n_dp,
    n_chain,
    ev_ref,
    dest_ref,
    hist_ref,
    ct_ref,
    wu_hbm,
    wo_hbm,
    layer_out_ref,
    event_grad_ref,
    weight_grad_ref,
    wu,
    wo,
    ev_send,
    ev_recv,
    residual_ref,
    normed_ref,
    pre_ref,
    gating_ref,
    gated_grad_ref,
    qkv_send,
    qkv,
    hist_col,
    att,
    slope,
    sgrad,
    mix_send,
    mix_recv,
    mg_send,
    mg,
    gated_ref,
    wg_send,
    wg_recv,
    d_send,
    d_recv,
    pg_ref,
    ng_ref,
    part_send,
    part_recv,
    full_send,
    full_recv,
    ret_send,
    ret_recv,
    load_sem,
    local_sem,
    ev_sems,
    wg_sems,
    ret_sems,
    qkv_ss,
    qkv_rs,
    mix_ss,
    mix_rs,
    mg_ss,
    mg_rs,
    d_ss,
    d_rs,
    part_ss,
    part_rs,
    full_ss,
    full_rs,
):
    rows, width = ev_ref.shape
    head = width // HEADS
    tokens = rows * n_chain
    per_peer = rows // n_dp
    fold = max(1, 16 // per_peer)
    block = per_peer * fold
    total = rows * fold
    cols = width // fold
    alpha = head ** (-0.5)
    share = width // n_dp
    e = lax.axis_index("dp")
    c = lax.axis_index("chain")

    load_wu = pltpu.make_async_copy(wu_hbm, wu, load_sem.at[0])
    load_wo = pltpu.make_async_copy(wo_hbm, wo, load_sem.at[1])
    load_wu.start()
    load_wo.start()

    barrier = pltpu.get_barrier_semaphore()

    def greet(step, carry):
        pl.semaphore_signal(
            barrier, inc=1, device_id=(lax.rem(e + step, n_dp), c), device_id_type=MESH
        )
        return carry

    lax.fori_loop(1, n_dp, greet, 0)
    for step in range(1, n_chain):
        pl.semaphore_signal(
            barrier, inc=1, device_id=(e, lax.rem(c + step, n_chain)), device_id_type=MESH
        )

    ri = iota((rows, rows), 0)
    ci = iota((rows, rows), 1)
    eye = ri == ci
    d_row = jnp.broadcast_to(dest_ref[...], (rows, rows))
    d_col = jnp.sum(jnp.where(eye, d_row.astype(F32), 0.0), axis=1, keepdims=True)
    d_col = jnp.broadcast_to(d_col, (rows, rows)).astype(I32)
    t_row = d_row // rows
    t_col = d_col // rows
    same = t_row == t_col
    rank_row = jnp.sum(jnp.where(same & (ri < ci), 1.0, 0.0), axis=0, keepdims=True)
    rank_col = jnp.sum(jnp.where(same & (ci < ri), 1.0, 0.0), axis=1, keepdims=True)
    place_row = block * t_row[:1, :] + rank_row.astype(I32)
    place_col = block * t_col + jnp.broadcast_to(rank_col, (rows, rows)).astype(I32)
    slots = (d_col - t_col * rows).astype(F32).astype(BF)
    at_row = jnp.broadcast_to(place_row, (total, rows))
    at = iota((total, rows), 0)
    spread = jnp.concatenate(
        [one_hot(at == at_row + per_peer * q) for q in range(fold)], axis=1
    )
    packed = jnp.concatenate(
        [
            jnp.concatenate([ev_ref[:, cols * q : cols * (q + 1)], slots], axis=1)
            for q in range(fold)
        ],
        axis=0,
    )
    ev_send[...] = dot(spread, packed).astype(BF)
    own_ev = pl.ds(pl.multiple_of(e * block, block), block)
    ev_recv[own_ev, :] = ev_send[own_ev, :]

    pl.semaphore_wait(barrier, n_dp - 1 + n_chain - 1)

    def to_group(send, recv, sems, rows_each):
        here = pl.ds(pl.multiple_of(e * rows_each, rows_each), rows_each)

        def one(step, carry):
            peer = lax.rem(e + step, n_dp)
            there = pl.ds(pl.multiple_of(peer * rows_each, rows_each), rows_each)
            pltpu.make_async_remote_copy(
                src_ref=send.at[there],
                dst_ref=recv.at[here],
                send_sem=sems.at[0],
                recv_sem=sems.at[1],
                device_id=(peer, c),
                device_id_type=MESH,
            ).start()
            return carry

        return one

    def await_group(buffer, sem, rows_each):
        part = buffer.at[pl.ds(0, (n_dp - 1) * rows_each)]
        pltpu.make_async_copy(part, part, sem).wait()

    lax.fori_loop(1, n_dp, to_group(ev_send, ev_recv, ev_sems, block), 0)

    for b in range(n_chain):
        ids = jnp.broadcast_to(
            hist_ref[:, rows * b : rows * (b + 1)].astype(F32), (rows, rows)
        )
        hist_col[rows * b : rows * (b + 1), :] = jnp.broadcast_to(
            jnp.sum(jnp.where(eye, ids, 0.0), axis=1, keepdims=True), (rows, rows)
        )

    await_group(ev_recv, ev_sems.at[1], block)
    slot_col = ev_recv[:, cols : cols + rows].astype(F32).astype(I32)
    slot_row = jnp.concatenate(
        [
            jnp.sum(
                jnp.where(eye, slot_col[rows * b : rows * (b + 1), :], 0).astype(F32),
                axis=0,
                keepdims=True,
            )
            for b in range(fold)
        ],
        axis=1,
    ).astype(I32)
    slot_row = jnp.broadcast_to(slot_row, (rows, total))
    slot_here = slot_row == iota((rows, total), 0)
    quarter = lax.rem(iota((rows, total), 1), block) // per_peer
    arrived = ev_recv[:, :cols]
    residual = jnp.concatenate(
        [dot(one_hot(slot_here & (quarter == q)), arrived) for q in range(fold)], axis=1
    )
    residual_ref[...] = residual
    center = residual - mean(residual)
    inverse = lax.rsqrt(mean(center * center) + epsilon)
    normed_ref[...] = (center * inverse).astype(BF)

    def chain_copy(src, dst, send_sem, recv_sem, peer):
        away = lax.rem(peer - c + n_chain, n_chain)
        return pltpu.make_async_remote_copy(
            src_ref=src,
            dst_ref=dst,
            send_sem=send_sem.at[away],
            recv_sem=recv_sem.at[away],
            device_id=(e, peer),
            device_id_type=MESH,
        )

    mine = pl.ds(pl.multiple_of(c * rows, rows), rows)

    load_wu.wait()
    for turn in (2, 1, 3, 0):
        pair = lax.rem(c // 2 + turn, n_chain // 2)
        for slot, part in ((0, 2), (1, 3), (2, 1)):
            columns = pl.ds(pl.multiple_of(part * width + pair * 2 * head, 2 * head), 2 * head)
            pre = dot(normed_ref[...], wu[:, columns])
            pre_ref[:, columns] = pre
            act = (pre * sigmoid(pre)).astype(BF)
            for b in range(2):
                qkv_send[2 * pair + b, :, slot * head : (slot + 1) * head] = act[
                    :, b * head : (b + 1) * head
                ]
        for b in range(2):
            peer = 2 * pair + b

            @pl.when(peer != c)
            def _(peer=peer):
                chain_copy(qkv_send.at[peer], qkv.at[mine], qkv_ss, qkv_rs, peer).start()

    qkv[mine, :] = qkv_send[c]

    pre = dot(normed_ref[...], wu[:, :width])
    sig = sigmoid(pre)
    gating_ref[...] = (pre * sig).astype(BF)
    pre_ref[:, :width] = sig * (1.0 + pre * (1.0 - sig))
    load_wo.wait()
    gated_grad_ref[...] = dot_nt(ct_ref[...], wo[...])

    def to_slope(step, carry):
        columns = pl.ds(pl.multiple_of(width + step * 512, 512), 512)
        v = pre_ref[:, columns]
        s = sigmoid(v)
        pre_ref[:, columns] = s * (1.0 + v * (1.0 - s))
        return carry

    lax.fori_loop(0, 3 * width // 512, to_slope, 0)

    def await_chain(src, dst, send_sem, recv_sem):
        for away in range(1, n_chain):
            pltpu.make_async_remote_copy(
                src_ref=src,
                dst_ref=dst,
                send_sem=send_sem.at[away],
                recv_sem=recv_sem.at[away],
                device_id=(e, c),
                device_id_type=MESH,
            ).wait_recv()

    def await_sent(src, dst, send_sem, recv_sem):
        for away in range(1, n_chain):
            pltpu.make_async_remote_copy(
                src_ref=src,
                dst_ref=dst,
                send_sem=send_sem.at[away],
                recv_sem=recv_sem.at[away],
                device_id=(e, c),
                device_id_type=MESH,
            ).wait_send()

    await_chain(qkv_send.at[0], qkv.at[pl.ds(0, rows)], qkv_ss, qkv_rs)

    tile = 2 * rows
    tiles = tokens // tile
    lower = iota((tile, tile), 0) >= iota((tile, tile), 1)
    for i in range(tiles):
        at_i = slice(tile * i, tile * (i + 1))
        ids = hist_col[at_i, :]
        ids = jnp.concatenate([ids, ids], axis=1)
        mixed = None
        for j in range(i + 1):
            at_j = slice(tile * j, tile * (j + 1))
            scores = dot_nt(qkv[at_i, :head], qkv[at_j, head : 2 * head]) * alpha
            visible = ids == hist_ref[:, at_j].astype(F32)
            if i == j:
                visible = visible & lower
            sig = sigmoid(scores)
            weights = jnp.where(visible, scores * sig, 0.0).astype(BF)
            att[at_i, at_j] = weights
            slope[at_i, at_j] = jnp.where(
                visible, (alpha * sig) * (1.0 + scores * (1.0 - sig)), 0.0
            )
            term = dot(weights, qkv[at_j, 2 * head :])
            mixed = term if mixed is None else mixed + term
        mix_send[at_i, :] = mixed.astype(BF)
        for b in range(2):
            peer = 2 * i + b

            @pl.when(peer != c)
            def _(peer=peer):
                chain_copy(
                    mix_send.at[pl.ds(peer * rows, rows)], mix_recv.at[c], mix_ss, mix_rs, peer
                ).start()

    mix_recv[c] = mix_send[mine, :]
    await_chain(mix_send.at[pl.ds(0, rows)], mix_recv.at[0], mix_ss, mix_rs)

    mixed = jnp.concatenate([mix_recv[h] for h in range(HEADS)], axis=1).astype(F32)
    center = mixed - mean(mixed)
    inverse = lax.rsqrt(mean(center * center) + epsilon)
    mixed_norm = center * inverse
    gating = gating_ref[...].astype(F32)
    gated_grad = gated_grad_ref[...]
    upstream = gated_grad * gating
    mixed_grad = inverse * (
        upstream - mean(upstream) - mixed_norm * mean(upstream * mixed_norm)
    )
    mixed_grad = mixed_grad.astype(BF)
    for h in range(HEADS):
        mg_send[h] = mixed_grad[:, h * head : (h + 1) * head]
    for away in (4, 3, 5, 2, 6, 1, 7):
        peer = lax.rem(c + away, n_chain)
        chain_copy(mg_send.at[peer], mg.at[mine], mg_ss, mg_rs, peer).start()
    mg[mine, :] = mg_send[c]
    gated_ref[...] = (mixed_norm * gating).astype(BF)
    pg_ref[:, :width] = (gated_grad * mixed_norm * pre_ref[:, :width]).astype(BF)

    grad_scale = 1.0 / math.sqrt(rows * n_dp * n_chain)

    def weight_term(step, carry):
        columns = pl.ds(pl.multiple_of(step * rows, rows), rows)
        wg_send[columns, :] = (
            dot_tn(gated_ref[:, columns], ct_ref[...]) * grad_scale
        ).astype(BF)
        return carry

    lax.fori_loop(0, width // rows, weight_term, 0)
    own_wg = pl.ds(pl.multiple_of(e * share, share), share)
    wg_recv[own_wg, :] = wg_send[own_wg, :]
    lax.fori_loop(1, n_dp, to_group(wg_send, wg_recv, wg_sems, share), 0)

    layer_out_ref[...] = (residual_ref[...] + dot(gated_ref[...], wo[...])).astype(BF)
    ng_ref[...] = dot_nt(pg_ref[:, :width], wu[:, :width])

    await_chain(mg_send.at[0], mg.at[pl.ds(0, rows)], mg_ss, mg_rs)

    for i in range(tiles - 1, -1, -1):
        at_i = slice(tile * i, tile * (i + 1))
        after = slice(tile * i, tokens)
        query_grad = None
        for j in range(i + 1):
            at_j = slice(tile * j, tile * (j + 1))
            grad = dot_nt(mg[at_i, :], qkv[at_j, 2 * head :])
            grad = (grad * slope[at_i, at_j]).astype(BF)
            sgrad[at_i, at_j] = grad
            term = dot(grad, qkv[at_j, head : 2 * head])
            query_grad = term if query_grad is None else query_grad + term
        key_grad = dot_tn(sgrad[after, at_i], qkv[after, :head])
        value_grad = dot_tn(att[after, at_i], mg[after, :])
        grads = jnp.concatenate([query_grad, key_grad, value_grad], axis=1).astype(BF)
        for b in range(2):
            peer = 2 * i + b
            d_send[peer] = grads[rows * b : rows * (b + 1), :]

            @pl.when(peer != c)
            def _(peer=peer):
                chain_copy(d_send.at[peer], d_recv.at[c], d_ss, d_rs, peer).start()

    d_recv[c] = d_send[c]

    await_group(wg_recv, wg_sems.at[1], share)

    def add_up(step, carry):
        here = pl.ds(pl.multiple_of(step * share, share), share)
        return carry + wg_recv[here, :].astype(F32)

    summed = lax.fori_loop(0, n_dp, add_up, jnp.zeros((share, width), F32)).astype(BF)
    for h in range(n_chain):
        part_send[h] = summed[:, h * head : (h + 1) * head]
    for away in (4, 3, 5, 2, 6, 1, 7):
        peer = lax.rem(c + away, n_chain)
        chain_copy(part_send.at[peer], part_recv.at[c], part_ss, part_rs, peer).start()
    part_recv[c] = part_send[c]

    await_chain(d_send.at[0], d_recv.at[0], d_ss, d_rs)
    for slot, part in ((0, 2), (1, 3), (2, 1)):
        for h in range(HEADS):
            columns = slice(part * width + h * head, part * width + (h + 1) * head)
            pg_ref[:, columns] = (
                d_recv[h, :, slot * head : (slot + 1) * head].astype(F32)
                * pre_ref[:, columns]
            ).astype(BF)
    normed_grad = ng_ref[...] + dot_nt(pg_ref[:, width:], wu[:, width:])

    await_chain(part_send.at[0], part_recv.at[0], part_ss, part_rs)
    whole = part_recv[0].astype(F32)
    for h in range(1, n_chain):
        whole = whole + part_recv[h].astype(F32)
    full_send[...] = whole.astype(BF)
    for away in (4, 3, 5, 2, 6, 1, 7):
        peer = lax.rem(c + away, n_chain)
        chain_copy(full_send, full_recv.at[c], full_ss, full_rs, peer).start()
    full_recv[c] = full_send[...]

    residual = residual_ref[...]
    center = residual - mean(residual)
    inverse = lax.rsqrt(mean(center * center) + epsilon)
    normed = center * inverse
    input_grad = ct_ref[...].astype(F32) + inverse * (
        normed_grad - mean(normed_grad) - normed * mean(normed_grad * normed)
    )
    input_grad = input_grad.astype(BF)

    slot_col = ev_recv[:, cols : cols + rows].astype(F32).astype(I32)
    slot_there = slot_col == iota((total, rows), 1)
    quarter = lax.rem(iota((total, rows), 0), block) // per_peer
    back = jnp.concatenate(
        [one_hot(slot_there & (quarter == q)) for q in range(fold)], axis=1
    )
    stacked = jnp.concatenate(
        [input_grad[:, cols * q : cols * (q + 1)] for q in range(fold)], axis=0
    )
    ret_send[...] = dot(back, stacked).astype(BF)
    ret_recv[own_ev, :] = ret_send[own_ev, :]
    lax.fori_loop(1, n_dp, to_group(ret_send, ret_recv, ret_sems, block), 0)

    await_chain(full_send, full_recv.at[0], full_ss, full_rs)
    for h in range(n_chain):
        weight_grad_ref[:, h * head : (h + 1) * head] = full_recv[h].astype(F32)

    await_group(ret_recv, ret_sems.at[1], block)
    returned = ret_recv[...]
    place = jnp.concatenate([place_col] * fold, axis=1)
    here = iota((rows, total), 1)
    for q in range(fold):
        event_grad_ref[:, cols * q : cols * (q + 1)] = dot(
            one_hot(here == place + per_peer * q), returned
        ).astype(BF)

    await_group(ev_send, ev_sems.at[0], block)
    await_group(wg_send, wg_sems.at[0], share)
    await_group(ret_send, ret_sems.at[0], block)
    await_sent(qkv_send.at[0], qkv.at[pl.ds(0, rows)], qkv_ss, qkv_rs)
    await_sent(mix_send.at[pl.ds(0, rows)], mix_recv.at[0], mix_ss, mix_rs)
    await_sent(mg_send.at[0], mg.at[pl.ds(0, rows)], mg_ss, mg_rs)
    await_sent(d_send.at[0], d_recv.at[0], d_ss, d_rs)
    await_sent(part_send.at[0], part_recv.at[0], part_ss, part_rs)
    await_sent(full_send, full_recv.at[0], full_ss, full_rs)


def on_device(n_dp, n_chain, events, destinations, history_ids, cotangent, w_uvqk, w_out):
    _, rows, width = events.shape
    head = width // HEADS
    tokens = rows * n_chain
    per_peer = rows // n_dp
    fold = max(1, 16 // per_peer)
    total = rows * fold
    cols = width // fold
    share = width // n_dp
    vmem = pl.BlockSpec(memory_space=pltpu.VMEM)
    anywhere = pl.BlockSpec(memory_space=pl.ANY)
    pair = pltpu.SemaphoreType.DMA((2,))
    ring = pltpu.SemaphoreType.DMA((n_chain,))
    layer_out, event_grad, weight_grad = pl.pallas_call(
        functools.partial(kernel, n_dp, n_chain),
        out_shape=(
            jax.ShapeDtypeStruct((rows, width), BF),
            jax.ShapeDtypeStruct((rows, width), BF),
            jax.ShapeDtypeStruct((share, width), F32),
        ),
        in_specs=[vmem, vmem, vmem, vmem, anywhere, anywhere],
        out_specs=(vmem, vmem, vmem),
        scratch_shapes=[
            pltpu.VMEM((width, 4 * width), BF),
            pltpu.VMEM((width, width), BF),
            pltpu.VMEM((total, cols + rows), BF),
            pltpu.VMEM((total, cols + rows), BF),
            pltpu.VMEM((rows, width), F32),
            pltpu.VMEM((rows, width), BF),
            pltpu.VMEM((rows, 4 * width), F32),
            pltpu.VMEM((rows, width), BF),
            pltpu.VMEM((rows, width), F32),
            pltpu.VMEM((n_chain, rows, 3 * head), BF),
            pltpu.VMEM((tokens, 3 * head), BF),
            pltpu.VMEM((tokens, rows), F32),
            pltpu.VMEM((tokens, tokens), BF),
            pltpu.VMEM((tokens, tokens), F32),
            pltpu.VMEM((tokens, tokens), BF),
            pltpu.VMEM((tokens, head), BF),
            pltpu.VMEM((n_chain, rows, head), BF),
            pltpu.VMEM((n_chain, rows, head), BF),
            pltpu.VMEM((tokens, head), BF),
            pltpu.VMEM((rows, width), BF),
            pltpu.VMEM((width, width), BF),
            pltpu.VMEM((width, width), BF),
            pltpu.VMEM((n_chain, rows, 3 * head), BF),
            pltpu.VMEM((n_chain, rows, 3 * head), BF),
            pltpu.VMEM((rows, 4 * width), BF),
            pltpu.VMEM((rows, width), F32),
            pltpu.VMEM((n_chain, share, head), BF),
            pltpu.VMEM((n_chain, share, head), BF),
            pltpu.VMEM((share, head), BF),
            pltpu.VMEM((n_chain, share, head), BF),
            pltpu.VMEM((total, cols), BF),
            pltpu.VMEM((total, cols), BF),
            pair,
            pair,
            pair,
            pair,
            pair,
        ]
        + [ring] * 12,
        compiler_params=pltpu.CompilerParams(
            collective_id=0, has_side_effects=True, vmem_limit_bytes=56 * 1024 * 1024
        ),
        cost_estimate=pl.CostEstimate(
            flops=9 * 2**30, bytes_accessed=12 * 2**20, transcendentals=4 * 2**20
        ),
        name="hstu_layer",
    )(events[0], destinations, history_ids, cotangent[0], w_uvqk, w_out)
    return (layer_out[None], event_grad[None], weight_grad)


def solution(mesh):
    return jax.shard_map(
        functools.partial(on_device, mesh.shape["dp"], mesh.shape["chain"]),
        mesh=mesh,
        in_specs=(
            P("dp", "chain", None),
            P("dp", "chain"),
            P("dp", None),
            P("dp", "chain", None),
            P(),
            P(),
        ),
        out_specs=(P("dp", "chain", None), P("dp", "chain", None), P("dp", None)),
        check_vma=False,
    )
```

```python
import functools
import math

import jax
import jax.numpy as jnp
from jax import lax
from jax.experimental import pallas as pl
from jax.experimental.pallas import tpu as pltpu
from jax.sharding import PartitionSpec as P

HEADS = 8
MESH = pl.DeviceIdType.MESH
BF = jnp.bfloat16
F32 = jnp.float32
I32 = jnp.int32
epsilon = 1e-05


def dot(a, b):
    return lax.dot_general(a, b, (((1,), (0,)), ((), ())), preferred_element_type=F32)


def dot_nt(a, b):
    return lax.dot_general(a, b, (((1,), (1,)), ((), ())), preferred_element_type=F32)


def dot_tn(a, b):
    return lax.dot_general(a, b, (((0,), (0,)), ((), ())), preferred_element_type=F32)


def sigmoid(v):
    return 0.5 * jnp.tanh(0.5 * v) + 0.5


def iota(shape, dim):
    return lax.broadcasted_iota(I32, shape, dim)


def mean(v):
    return jnp.mean(v, axis=-1, keepdims=True)


def one_hot(mask):
    return jnp.where(mask, 1.0, 0.0).astype(BF)


def kernel(
    n_dp,
    n_chain,
    dest_ref,
    hist_ref,
    ev_hbm,
    ct_hbm,
    wu_hbm,
    wo_hbm,
    event_grad_ref,
    layer_out_hbm,
    weight_grad_hbm,
    ev_ref,
    ct_ref,
    layer_out_ref,
    weight_grad_ref,
    wu,
    wo,
    ev_send,
    ev_recv,
    residual_ref,
    normed_ref,
    pre_ref,
    gating_ref,
    gated_grad_ref,
    qkv_send,
    qkv,
    hist_col,
    att,
    slope,
    sgrad,
    mix_send,
    mix_recv,
    mg_send,
    mg,
    gated_ref,
    wg_send,
    wg_twin,
    wg_recv,
    d_send,
    d_recv,
    pg_ref,
    ng_ref,
    part_send,
    part_recv,
    full_send,
    full_recv,
    ret_send,
    ret_recv,
    load_sem,
    store_sem,
    ev_sems,
    twin_sems,
    wg_sems,
    ret_sems,
    qkv_ss,
    qkv_rs,
    mix_ss,
    mix_rs,
    mg_ss,
    mg_rs,
    d_ss,
    d_rs,
    part_ss,
    part_rs,
    full_ss,
    full_rs,
):
    rows, width = ev_ref.shape
    head = width // HEADS
    tokens = rows * n_chain
    per_peer = rows // n_dp
    fold = max(1, 16 // per_peer)
    block = per_peer * fold
    total = rows * fold
    cols = width // fold
    alpha = head ** (-0.5)
    share = width // n_dp
    e = lax.axis_index("dp")
    c = lax.axis_index("chain")

    load_ev = pltpu.make_async_copy(ev_hbm, ev_ref, load_sem.at[2])
    load_ct = pltpu.make_async_copy(ct_hbm, ct_ref, load_sem.at[3])
    load_wu = pltpu.make_async_copy(wu_hbm, wu, load_sem.at[0])
    load_wo = pltpu.make_async_copy(wo_hbm, wo, load_sem.at[1])
    load_ev.start()

    barrier = pltpu.get_barrier_semaphore()

    def greet(step, carry):
        pl.semaphore_signal(
            barrier, inc=1, device_id=(lax.rem(e + step, n_dp), c), device_id_type=MESH
        )
        return carry

    lax.fori_loop(1, n_dp, greet, 0)
    for step in range(1, n_chain):
        pl.semaphore_signal(
            barrier, inc=1, device_id=(e, lax.rem(c + step, n_chain)), device_id_type=MESH
        )

    load_wu.start()
    load_ct.start()
    load_wo.start()

    ri = iota((rows, rows), 0)
    ci = iota((rows, rows), 1)
    eye = ri == ci
    d_row = jnp.broadcast_to(dest_ref[...], (rows, rows))
    d_col = jnp.sum(jnp.where(eye, d_row.astype(F32), 0.0), axis=1, keepdims=True)
    d_col = jnp.broadcast_to(d_col, (rows, rows)).astype(I32)
    t_row = d_row // rows
    t_col = d_col // rows
    same = t_row == t_col
    rank_row = jnp.sum(jnp.where(same & (ri < ci), 1.0, 0.0), axis=0, keepdims=True)
    rank_col = jnp.sum(jnp.where(same & (ci < ri), 1.0, 0.0), axis=1, keepdims=True)
    place_row = block * t_row[:1, :] + rank_row.astype(I32)
    place_col = block * t_col + jnp.broadcast_to(rank_col, (rows, rows)).astype(I32)
    slots = (d_col - t_col * rows).astype(F32).astype(BF)
    at_row = jnp.broadcast_to(place_row, (total, rows))
    at = iota((total, rows), 0)
    spread = jnp.concatenate(
        [one_hot(at == at_row + per_peer * q) for q in range(fold)], axis=1
    )
    load_ev.wait()
    packed = jnp.concatenate(
        [
            jnp.concatenate([ev_ref[:, cols * q : cols * (q + 1)], slots], axis=1)
            for q in range(fold)
        ],
        axis=0,
    )
    ev_send[...] = dot(spread, packed).astype(BF)
    own_ev = pl.ds(pl.multiple_of(e * block, block), block)
    ev_recv[own_ev, :] = ev_send[own_ev, :]

    pl.semaphore_wait(barrier, n_dp - 1 + n_chain - 1)

    def to_group(send, recv, sems, rows_each):
        here = pl.ds(pl.multiple_of(e * rows_each, rows_each), rows_each)

        def one(step, carry):
            peer = lax.rem(e + step, n_dp)
            there = pl.ds(pl.multiple_of(peer * rows_each, rows_each), rows_each)
            pltpu.make_async_remote_copy(
                src_ref=send.at[there],
                dst_ref=recv.at[here],
                send_sem=sems.at[0],
                recv_sem=sems.at[1],
                device_id=(peer, c),
                device_id_type=MESH,
            ).start()
            return carry

        return one

    def await_group(buffer, sem, rows_each, peers=n_dp - 1):
        part = buffer.at[pl.ds(0, peers * rows_each)]
        pltpu.make_async_copy(part, part, sem).wait()

    lax.fori_loop(1, n_dp, to_group(ev_send, ev_recv, ev_sems, block), 0)

    for b in range(n_chain):
        ids = jnp.broadcast_to(
            hist_ref[:, rows * b : rows * (b + 1)].astype(F32), (rows, rows)
        )
        hist_col[rows * b : rows * (b + 1), :] = jnp.broadcast_to(
            jnp.sum(jnp.where(eye, ids, 0.0), axis=1, keepdims=True), (rows, rows)
        )

    await_group(ev_recv, ev_sems.at[1], block)
    slot_col = ev_recv[:, cols : cols + rows].astype(F32).astype(I32)
    slot_row = jnp.concatenate(
        [
            jnp.sum(
                jnp.where(eye, slot_col[rows * b : rows * (b + 1), :], 0).astype(F32),
                axis=0,
                keepdims=True,
            )
            for b in range(fold)
        ],
        axis=1,
    ).astype(I32)
    slot_row = jnp.broadcast_to(slot_row, (rows, total))
    slot_here = slot_row == iota((rows, total), 0)
    quarter = lax.rem(iota((rows, total), 1), block) // per_peer
    arrived = ev_recv[:, :cols]
    residual = jnp.concatenate(
        [dot(one_hot(slot_here & (quarter == q)), arrived) for q in range(fold)], axis=1
    )
    residual_ref[...] = residual
    center = residual - mean(residual)
    inverse = lax.rsqrt(mean(center * center) + epsilon)
    normed_ref[...] = (center * inverse).astype(BF)

    def chain_copy(src, dst, send_sem, recv_sem, peer):
        away = lax.rem(peer - c + n_chain, n_chain)
        return pltpu.make_async_remote_copy(
            src_ref=src,
            dst_ref=dst,
            send_sem=send_sem.at[away],
            recv_sem=recv_sem.at[away],
            device_id=(e, peer),
            device_id_type=MESH,
        )

    mine = pl.ds(pl.multiple_of(c * rows, rows), rows)

    load_wu.wait()
    for turn in (2, 1, 3, 0):
        pair = lax.rem(c // 2 + turn, n_chain // 2)
        for slot, part in ((0, 2), (1, 3), (2, 1)):
            columns = pl.ds(pl.multiple_of(part * width + pair * 2 * head, 2 * head), 2 * head)
            pre = dot(normed_ref[...], wu[:, columns])
            pre_ref[:, columns] = pre
            act = (pre * sigmoid(pre)).astype(BF)
            for b in range(2):
                qkv_send[2 * pair + b, :, slot * head : (slot + 1) * head] = act[
                    :, b * head : (b + 1) * head
                ]
        for b in range(2):
            peer = 2 * pair + b

            @pl.when(peer != c)
            def _(peer=peer):
                chain_copy(qkv_send.at[peer], qkv.at[mine], qkv_ss, qkv_rs, peer).start()

    qkv[mine, :] = qkv_send[c]

    pre = dot(normed_ref[...], wu[:, :width])
    sig = sigmoid(pre)
    gating_ref[...] = (pre * sig).astype(BF)
    pre_ref[:, :width] = sig * (1.0 + pre * (1.0 - sig))
    load_wo.wait()
    load_ct.wait()
    gated_grad_ref[...] = dot_nt(ct_ref[...], wo[...])

    def to_slope(step, carry):
        columns = pl.ds(pl.multiple_of(width + step * 512, 512), 512)
        v = pre_ref[:, columns]
        s = sigmoid(v)
        pre_ref[:, columns] = s * (1.0 + v * (1.0 - s))
        return carry

    lax.fori_loop(0, 3 * width // 512, to_slope, 0)

    def await_chain(src, dst, send_sem, recv_sem):
        for away in range(1, n_chain):
            pltpu.make_async_remote_copy(
                src_ref=src,
                dst_ref=dst,
                send_sem=send_sem.at[away],
                recv_sem=recv_sem.at[away],
                device_id=(e, c),
                device_id_type=MESH,
            ).wait_recv()

    def await_sent(src, dst, send_sem, recv_sem):
        for away in range(1, n_chain):
            pltpu.make_async_remote_copy(
                src_ref=src,
                dst_ref=dst,
                send_sem=send_sem.at[away],
                recv_sem=recv_sem.at[away],
                device_id=(e, c),
                device_id_type=MESH,
            ).wait_send()

    await_chain(qkv_send.at[0], qkv.at[pl.ds(0, rows)], qkv_ss, qkv_rs)

    tile = 2 * rows
    tiles = tokens // tile
    lower = iota((tile, tile), 0) >= iota((tile, tile), 1)
    for i in range(tiles):
        at_i = slice(tile * i, tile * (i + 1))
        ids = hist_col[at_i, :]
        ids = jnp.concatenate([ids, ids], axis=1)
        mixed = None
        for j in range(i + 1):
            at_j = slice(tile * j, tile * (j + 1))
            scores = dot_nt(qkv[at_i, :head], qkv[at_j, head : 2 * head]) * alpha
            visible = ids == hist_ref[:, at_j].astype(F32)
            if i == j:
                visible = visible & lower
            sig = sigmoid(scores)
            weights = jnp.where(visible, scores * sig, 0.0).astype(BF)
            att[at_i, at_j] = weights
            slope[at_i, at_j] = jnp.where(
                visible, (alpha * sig) * (1.0 + scores * (1.0 - sig)), 0.0
            )
            term = dot(weights, qkv[at_j, 2 * head :])
            mixed = term if mixed is None else mixed + term
        mix_send[at_i, :] = mixed.astype(BF)
        for b in range(2):
            peer = 2 * i + b

            @pl.when(peer != c)
            def _(peer=peer):
                chain_copy(
                    mix_send.at[pl.ds(peer * rows, rows)], mix_recv.at[c], mix_ss, mix_rs, peer
                ).start()

    mix_recv[c] = mix_send[mine, :]
    await_chain(mix_send.at[pl.ds(0, rows)], mix_recv.at[0], mix_ss, mix_rs)

    mixed = jnp.concatenate([mix_recv[h] for h in range(HEADS)], axis=1).astype(F32)
    center = mixed - mean(mixed)
    inverse = lax.rsqrt(mean(center * center) + epsilon)
    mixed_norm = center * inverse
    gating = gating_ref[...].astype(F32)
    gated_grad = gated_grad_ref[...]
    upstream = gated_grad * gating
    mixed_grad = inverse * (
        upstream - mean(upstream) - mixed_norm * mean(upstream * mixed_norm)
    )
    mixed_grad = mixed_grad.astype(BF)
    for h in range(HEADS):
        mg_send[h] = mixed_grad[:, h * head : (h + 1) * head]
    for away in (4, 3, 5, 2, 6, 1, 7):
        peer = lax.rem(c + away, n_chain)
        chain_copy(mg_send.at[peer], mg.at[mine], mg_ss, mg_rs, peer).start()
    mg[mine, :] = mg_send[c]
    gated_ref[...] = (mixed_norm * gating).astype(BF)
    pg_ref[:, :width] = (gated_grad * mixed_norm * pre_ref[:, :width]).astype(BF)

    grad_scale = 1.0 / math.sqrt(rows * n_dp * n_chain)

    def weight_term(step, carry):
        columns = pl.ds(pl.multiple_of(step * 4 * share, 4 * share), 4 * share)
        term = (dot_tn(gated_ref[:, columns], ct_ref[...]) * grad_scale).astype(BF)
        for b in range(4):
            to = pl.ds(pl.multiple_of((2 * step + b // 2) * share, share), share)
            wg_send[b % 2, to, :] = term[b * share : (b + 1) * share, :]
        return carry

    lax.fori_loop(0, n_dp // 4, weight_term, 0)
    core = lax.rem(e, 2)
    twin_copy = pltpu.make_async_remote_copy(
        src_ref=wg_send.at[1 - core],
        dst_ref=wg_twin,
        send_sem=twin_sems.at[0],
        recv_sem=twin_sems.at[1],
        device_id=(e + 1 - 2 * core, c),
        device_id_type=MESH,
    )
    twin_copy.start()

    layer_out_ref[...] = (residual_ref[...] + dot(gated_ref[...], wo[...])).astype(BF)
    store_lo = pltpu.make_async_copy(layer_out_ref, layer_out_hbm, store_sem.at[0])
    store_lo.start()
    ng_ref[...] = dot_nt(pg_ref[:, :width], wu[:, :width])

    twin_copy.wait_recv()
    place_wg = e // 2

    def add_twin(step, carry):
        here = pl.ds(pl.multiple_of(step * share, share), share)
        wg_twin[here, :] = (
            wg_twin[here, :].astype(F32) + wg_send[core, here, :].astype(F32)
        ).astype(BF)
        return carry

    lax.fori_loop(0, n_dp // 2, add_twin, 0)
    own_wg = pl.ds(pl.multiple_of(place_wg * share, share), share)
    wg_recv[own_wg, :] = wg_twin[own_wg, :]

    def scatter(step, carry):
        peer = lax.rem(e + 2 * step, n_dp)
        there = pl.ds(pl.multiple_of(peer // 2 * share, share), share)
        pltpu.make_async_remote_copy(
            src_ref=wg_twin.at[there],
            dst_ref=wg_recv.at[own_wg],
            send_sem=wg_sems.at[0],
            recv_sem=wg_sems.at[1],
            device_id=(peer, c),
            device_id_type=MESH,
        ).start()
        return carry

    lax.fori_loop(1, n_dp // 2, scatter, 0)

    await_chain(mg_send.at[0], mg.at[pl.ds(0, rows)], mg_ss, mg_rs)

    for i in range(tiles - 1, -1, -1):
        at_i = slice(tile * i, tile * (i + 1))
        after = slice(tile * i, tokens)
        query_grad = None
        for j in range(i + 1):
            at_j = slice(tile * j, tile * (j + 1))
            grad = dot_nt(mg[at_i, :], qkv[at_j, 2 * head :])
            grad = (grad * slope[at_i, at_j]).astype(BF)
            sgrad[at_i, at_j] = grad
            term = dot(grad, qkv[at_j, head : 2 * head])
            query_grad = term if query_grad is None else query_grad + term
        key_grad = dot_tn(sgrad[after, at_i], qkv[after, :head])
        value_grad = dot_tn(att[after, at_i], mg[after, :])
        grads = jnp.concatenate([query_grad, key_grad, value_grad], axis=1).astype(BF)
        for b in range(2):
            peer = 2 * i + b
            d_send[peer] = grads[rows * b : rows * (b + 1), :]

            @pl.when(peer != c)
            def _(peer=peer):
                chain_copy(d_send.at[peer], d_recv.at[c], d_ss, d_rs, peer).start()

    d_recv[c] = d_send[c]

    await_group(wg_recv, wg_sems.at[1], share, n_dp // 2 - 1)

    def add_up(step, carry):
        here = pl.ds(pl.multiple_of(step * share, share), share)
        return carry + wg_recv[here, :].astype(F32)

    summed = lax.fori_loop(0, n_dp // 2, add_up, jnp.zeros((share, width), F32)).astype(BF)
    for h in range(n_chain):
        part_send[h] = summed[:, h * head : (h + 1) * head]
    for away in (4, 3, 5, 2, 6, 1, 7):
        peer = lax.rem(c + away, n_chain)
        chain_copy(part_send.at[peer], part_recv.at[c], part_ss, part_rs, peer).start()
    part_recv[c] = part_send[c]

    await_chain(d_send.at[0], d_recv.at[0], d_ss, d_rs)
    for slot, part in ((0, 2), (1, 3), (2, 1)):
        for h in range(HEADS):
            columns = slice(part * width + h * head, part * width + (h + 1) * head)
            pg_ref[:, columns] = (
                d_recv[h, :, slot * head : (slot + 1) * head].astype(F32)
                * pre_ref[:, columns]
            ).astype(BF)
    normed_grad = ng_ref[...] + dot_nt(pg_ref[:, width:], wu[:, width:])

    await_chain(part_send.at[0], part_recv.at[0], part_ss, part_rs)
    whole = part_recv[0].astype(F32)
    for h in range(1, n_chain):
        whole = whole + part_recv[h].astype(F32)
    full_send[...] = whole.astype(BF)
    for away in (4, 3, 5, 2, 6, 1, 7):
        peer = lax.rem(c + away, n_chain)
        chain_copy(full_send, full_recv.at[c], full_ss, full_rs, peer).start()
    full_recv[c] = full_send[...]

    residual = residual_ref[...]
    center = residual - mean(residual)
    inverse = lax.rsqrt(mean(center * center) + epsilon)
    normed = center * inverse
    input_grad = ct_ref[...].astype(F32) + inverse * (
        normed_grad - mean(normed_grad) - normed * mean(normed_grad * normed)
    )
    input_grad = input_grad.astype(BF)

    slot_col = ev_recv[:, cols : cols + rows].astype(F32).astype(I32)
    slot_there = slot_col == iota((total, rows), 1)
    quarter = lax.rem(iota((total, rows), 0), block) // per_peer
    back = jnp.concatenate(
        [one_hot(slot_there & (quarter == q)) for q in range(fold)], axis=1
    )
    stacked = jnp.concatenate(
        [input_grad[:, cols * q : cols * (q + 1)] for q in range(fold)], axis=0
    )
    ret_send[...] = dot(back, stacked).astype(BF)
    ret_recv[own_ev, :] = ret_send[own_ev, :]
    lax.fori_loop(1, n_dp, to_group(ret_send, ret_recv, ret_sems, block), 0)

    await_chain(full_send, full_recv.at[0], full_ss, full_rs)
    for h in range(n_chain):
        weight_grad_ref[:, h * head : (h + 1) * head] = full_recv[h].astype(F32)
    store_wg = pltpu.make_async_copy(weight_grad_ref, weight_grad_hbm, store_sem.at[1])
    store_wg.start()

    await_group(ret_recv, ret_sems.at[1], block)
    returned = ret_recv[...]
    place = jnp.concatenate([place_col] * fold, axis=1)
    here = iota((rows, total), 1)
    for q in range(fold):
        event_grad_ref[:, cols * q : cols * (q + 1)] = dot(
            one_hot(here == place + per_peer * q), returned
        ).astype(BF)

    await_group(ev_send, ev_sems.at[0], block)
    await_group(wg_twin, wg_sems.at[0], share, n_dp // 2 - 1)
    twin_copy.wait_send()
    await_group(ret_send, ret_sems.at[0], block)
    await_sent(qkv_send.at[0], qkv.at[pl.ds(0, rows)], qkv_ss, qkv_rs)
    await_sent(mix_send.at[pl.ds(0, rows)], mix_recv.at[0], mix_ss, mix_rs)
    await_sent(mg_send.at[0], mg.at[pl.ds(0, rows)], mg_ss, mg_rs)
    await_sent(d_send.at[0], d_recv.at[0], d_ss, d_rs)
    await_sent(part_send.at[0], part_recv.at[0], part_ss, part_rs)
    await_sent(full_send, full_recv.at[0], full_ss, full_rs)
    store_lo.wait()
    store_wg.wait()


def hand_over(a, b, c, a_out, b_out, c_out):
    a_out[...] = a[...]
    b_out[...] = b[...]
    c_out[...] = c[...]


def on_device(n_dp, n_chain, events, destinations, history_ids, cotangent, w_uvqk, w_out):
    _, rows, width = events.shape
    head = width // HEADS
    tokens = rows * n_chain
    per_peer = rows // n_dp
    fold = max(1, 16 // per_peer)
    total = rows * fold
    cols = width // fold
    share = width // n_dp
    vmem = pl.BlockSpec(memory_space=pltpu.VMEM)
    anywhere = pl.BlockSpec(memory_space=pl.ANY)
    pair = pltpu.SemaphoreType.DMA((2,))
    ring = pltpu.SemaphoreType.DMA((n_chain,))
    results = pl.pallas_call(
        functools.partial(kernel, n_dp, n_chain),
        out_shape=(
            jax.ShapeDtypeStruct((rows, width), BF),
            jax.ShapeDtypeStruct((rows, width), BF),
            jax.ShapeDtypeStruct((share, width), F32),
        ),
        in_specs=[vmem, vmem, anywhere, anywhere, anywhere, anywhere],
        out_specs=(vmem, anywhere, anywhere),
        scratch_shapes=[
            pltpu.VMEM((rows, width), BF),
            pltpu.VMEM((rows, width), BF),
            pltpu.VMEM((rows, width), BF),
            pltpu.VMEM((share, width), F32),
            pltpu.VMEM((width, 4 * width), BF),
            pltpu.VMEM((width, width), BF),
            pltpu.VMEM((total, cols + rows), BF),
            pltpu.VMEM((total, cols + rows), BF),
            pltpu.VMEM((rows, width), F32),
            pltpu.VMEM((rows, width), BF),
            pltpu.VMEM((rows, 4 * width), F32),
            pltpu.VMEM((rows, width), BF),
            pltpu.VMEM((rows, width), F32),
            pltpu.VMEM((n_chain, rows, 3 * head), BF),
            pltpu.VMEM((tokens, 3 * head), BF),
            pltpu.VMEM((tokens, rows), F32),
            pltpu.VMEM((tokens, tokens), BF),
            pltpu.VMEM((tokens, tokens), F32),
            pltpu.VMEM((tokens, tokens), BF),
            pltpu.VMEM((tokens, head), BF),
            pltpu.VMEM((n_chain, rows, head), BF),
            pltpu.VMEM((n_chain, rows, head), BF),
            pltpu.VMEM((tokens, head), BF),
            pltpu.VMEM((rows, width), BF),
            pltpu.VMEM((2, width // 2, width), BF),
            pltpu.VMEM((width // 2, width), BF),
            pltpu.VMEM((width // 2, width), BF),
            pltpu.VMEM((n_chain, rows, 3 * head), BF),
            pltpu.VMEM((n_chain, rows, 3 * head), BF),
            pltpu.VMEM((rows, 4 * width), BF),
            pltpu.VMEM((rows, width), F32),
            pltpu.VMEM((n_chain, share, head), BF),
            pltpu.VMEM((n_chain, share, head), BF),
            pltpu.VMEM((share, head), BF),
            pltpu.VMEM((n_chain, share, head), BF),
            pltpu.VMEM((total, cols), BF),
            pltpu.VMEM((total, cols), BF),
            pltpu.SemaphoreType.DMA((4,)),
            pair,
            pair,
            pair,
            pair,
            pair,
        ]
        + [ring] * 12,
        compiler_params=pltpu.CompilerParams(
            collective_id=0, has_side_effects=True, vmem_limit_bytes=56 * 1024 * 1024
        ),
        cost_estimate=pl.CostEstimate(
            flops=9 * 2**30, bytes_accessed=12 * 2**20, transcendentals=4 * 2**20
        ),
        name="hstu_layer",
    )(destinations, history_ids, events[0], cotangent[0], w_uvqk, w_out)
    event_grad, layer_out, weight_grad = pl.pallas_call(
        hand_over,
        out_shape=tuple(jax.ShapeDtypeStruct(r.shape, r.dtype) for r in results),
        in_specs=[vmem] * 3,
        out_specs=(vmem,) * 3,
        name="hand_over",
    )(*results)
    return (layer_out[None], event_grad[None], weight_grad)


def solution(mesh):
    return jax.shard_map(
        functools.partial(on_device, mesh.shape["dp"], mesh.shape["chain"]),
        mesh=mesh,
        in_specs=(
            P("dp", "chain", None),
            P("dp", "chain"),
            P("dp", None),
            P("dp", "chain", None),
            P(),
            P(),
        ),
        out_specs=(P("dp", "chain", None), P("dp", "chain", None), P("dp", None)),
        check_vma=False,
    )
```

```python
import functools
import math

import jax
import jax.numpy as jnp
from jax import lax
from jax.experimental import pallas as pl
from jax.experimental.pallas import tpu as pltpu
from jax.sharding import PartitionSpec as P

HEADS = 8
MESH = pl.DeviceIdType.MESH
BF = jnp.bfloat16
F32 = jnp.float32
I32 = jnp.int32
epsilon = 1e-05


def dot(a, b):
    return lax.dot_general(a, b, (((1,), (0,)), ((), ())), preferred_element_type=F32)


def dot_nt(a, b):
    return lax.dot_general(a, b, (((1,), (1,)), ((), ())), preferred_element_type=F32)


def dot_tn(a, b):
    return lax.dot_general(a, b, (((0,), (0,)), ((), ())), preferred_element_type=F32)


def sigmoid(v):
    return 0.5 * jnp.tanh(0.5 * v) + 0.5


def iota(shape, dim):
    return lax.broadcasted_iota(I32, shape, dim)


def mean(v):
    return jnp.mean(v, axis=-1, keepdims=True)


def one_hot(mask):
    return jnp.where(mask, 1.0, 0.0).astype(BF)


def kernel(
    n_dp,
    n_chain,
    dest_ref,
    hist_ref,
    ev_hbm,
    ct_hbm,
    wu_hbm,
    wo_hbm,
    event_grad_ref,
    layer_out_hbm,
    weight_grad_hbm,
    ev_ref,
    ct_all,
    layer_out_ref,
    weight_grad_ref,
    wu,
    wo,
    ev_send,
    ev_recv,
    residual_ref,
    normed_ref,
    pre_ref,
    gating_ref,
    gated_grad_ref,
    qkv_send,
    qkv,
    hist_col,
    att,
    slope,
    sgrad,
    mix_send,
    mix_recv,
    h_send,
    h_recv,
    stat_send,
    stat_recv,
    mix_t,
    key_t,
    value_t,
    mg_t,
    mg,
    gated_ref,
    gt_send,
    gt_recv,
    wg_send,
    wg_recv,
    d_send,
    d_recv,
    pg_ref,
    ng_ref,
    part_send,
    part_recv,
    full_send,
    full_recv,
    back_ref,
    home_ref,
    inverse_ref,
    ret_send,
    ret_recv,
    load_sem,
    store_sem,
    ev_sems,
    ct_sems,
    gt_sems,
    wg_ss,
    wg_rs,
    ret_sems,
    qkv_ss,
    qkv_rs,
    mix_ss,
    mix_rs,
    h_ss,
    h_rs,
    stat_ss,
    stat_rs,
    d_ss,
    d_rs,
    part_ss,
    part_rs,
    full_ss,
    full_rs,
):
    rows, width = ev_ref.shape
    head = width // HEADS
    tokens = rows * n_chain
    per_peer = rows // n_dp
    fold = max(1, 16 // per_peer)
    block = per_peer * fold
    total = rows * fold
    cols = width // fold
    alpha = head ** (-0.5)
    share = width // n_dp
    e = lax.axis_index("dp")
    c = lax.axis_index("chain")
    team = width // rows
    teams = n_dp // team
    seat = lax.rem(e, team)
    ct_ref = ct_all.at[pl.ds(pl.multiple_of(seat * rows, rows), rows)]

    load_ev = pltpu.make_async_copy(ev_hbm, ev_ref, load_sem.at[2])
    load_ct = pltpu.make_async_copy(ct_hbm, ct_ref, load_sem.at[3])
    load_wu = pltpu.make_async_copy(wu_hbm, wu, load_sem.at[0])
    load_wo = pltpu.make_async_copy(wo_hbm, wo, load_sem.at[1])
    load_ev.start()

    barrier = pltpu.get_barrier_semaphore()

    def greet(step, carry):
        pl.semaphore_signal(
            barrier, inc=1, device_id=(lax.rem(e + step, n_dp), c), device_id_type=MESH
        )
        return carry

    lax.fori_loop(1, n_dp, greet, 0)
    for step in range(1, n_chain):
        pl.semaphore_signal(
            barrier, inc=1, device_id=(e, lax.rem(c + step, n_chain)), device_id_type=MESH
        )

    load_wu.start()
    load_ct.start()
    load_wo.start()

    ri = iota((rows, rows), 0)
    ci = iota((rows, rows), 1)
    eye = ri == ci
    d_row = jnp.broadcast_to(dest_ref[...], (rows, rows))
    d_col = jnp.sum(jnp.where(eye, d_row.astype(F32), 0.0), axis=1, keepdims=True)
    d_col = jnp.broadcast_to(d_col, (rows, rows)).astype(I32)
    t_row = d_row // rows
    t_col = d_col // rows
    same = t_row == t_col
    rank_row = jnp.sum(jnp.where(same & (ri < ci), 1.0, 0.0), axis=0, keepdims=True)
    rank_col = jnp.sum(jnp.where(same & (ci < ri), 1.0, 0.0), axis=1, keepdims=True)
    place_row = block * t_row[:1, :] + rank_row.astype(I32)
    place_col = block * t_col + jnp.broadcast_to(rank_col, (rows, rows)).astype(I32)
    slots = (d_col - t_col * rows).astype(F32).astype(BF)
    at_row = jnp.broadcast_to(place_row, (total, rows))
    at = iota((total, rows), 0)
    spread = jnp.concatenate(
        [one_hot(at == at_row + per_peer * q) for q in range(fold)], axis=1
    )
    load_ev.wait()
    packed = jnp.concatenate(
        [
            jnp.concatenate([ev_ref[:, cols * q : cols * (q + 1)], slots], axis=1)
            for q in range(fold)
        ],
        axis=0,
    )
    ev_send[...] = dot(spread, packed).astype(BF)
    own_ev = pl.ds(pl.multiple_of(e * block, block), block)
    ev_recv[own_ev, :] = ev_send[own_ev, :]

    pl.semaphore_wait(barrier, n_dp - 1 + n_chain - 1)

    def to_group(send, recv, sems, rows_each):
        here = pl.ds(pl.multiple_of(e * rows_each, rows_each), rows_each)

        def one(step, carry):
            peer = lax.rem(e + step, n_dp)
            there = pl.ds(pl.multiple_of(peer * rows_each, rows_each), rows_each)
            pltpu.make_async_remote_copy(
                src_ref=send.at[there],
                dst_ref=recv.at[here],
                send_sem=sems.at[0],
                recv_sem=sems.at[1],
                device_id=(peer, c),
                device_id_type=MESH,
            ).start()
            return carry

        return one

    def await_group(buffer, sem, rows_each, peers=n_dp - 1):
        part = buffer.at[pl.ds(0, peers * rows_each)]
        pltpu.make_async_copy(part, part, sem).wait()

    lax.fori_loop(1, n_dp, to_group(ev_send, ev_recv, ev_sems, block), 0)

    for b in range(n_chain):
        ids = jnp.broadcast_to(
            hist_ref[:, rows * b : rows * (b + 1)].astype(F32), (rows, rows)
        )
        hist_col[rows * b : rows * (b + 1), :] = jnp.broadcast_to(
            jnp.sum(jnp.where(eye, ids, 0.0), axis=1, keepdims=True), (rows, rows)
        )

    def to_team(src, dst, sems):
        for step in range(1, team):
            other = lax.rem(seat + step, team)
            pltpu.make_async_remote_copy(
                src_ref=src(other),
                dst_ref=dst,
                send_sem=sems.at[0],
                recv_sem=sems.at[1],
                device_id=(e - seat + other, c),
                device_id_type=MESH,
            ).start()

    await_group(ev_recv, ev_sems.at[1], block)
    load_ct.wait()
    slot_col = ev_recv[:, cols : cols + rows].astype(F32).astype(I32)
    slot_row = jnp.concatenate(
        [
            jnp.sum(
                jnp.where(eye, slot_col[rows * b : rows * (b + 1), :], 0).astype(F32),
                axis=0,
                keepdims=True,
            )
            for b in range(fold)
        ],
        axis=1,
    ).astype(I32)
    slot_row = jnp.broadcast_to(slot_row, (rows, total))
    slot_here = slot_row == iota((rows, total), 0)
    quarter = lax.rem(iota((rows, total), 1), block) // per_peer
    arrived = ev_recv[:, :cols]
    residual = jnp.concatenate(
        [dot(one_hot(slot_here & (quarter == q)), arrived) for q in range(fold)], axis=1
    )
    residual_ref[...] = residual
    center = residual - mean(residual)
    inverse = lax.rsqrt(mean(center * center) + epsilon)
    normed_ref[...] = (center * inverse).astype(BF)

    def chain_copy(src, dst, send_sem, recv_sem, peer):
        away = lax.rem(peer - c + n_chain, n_chain)
        return pltpu.make_async_remote_copy(
            src_ref=src,
            dst_ref=dst,
            send_sem=send_sem.at[away],
            recv_sem=recv_sem.at[away],
            device_id=(e, peer),
            device_id_type=MESH,
        )

    mine = pl.ds(pl.multiple_of(c * rows, rows), rows)

    load_wu.wait()
    for turn in (2, 1, 3, 0):
        pair = lax.rem(c // 2 + turn, n_chain // 2)
        for slot, part in ((0, 2), (1, 3), (2, 1)):
            columns = pl.ds(pl.multiple_of(part * width + pair * 2 * head, 2 * head), 2 * head)
            pre = dot(normed_ref[...], wu[:, columns])
            pre_ref[:, columns] = pre
            act = (pre * sigmoid(pre)).astype(BF)
            for b in range(2):
                qkv_send[2 * pair + b, :, slot * head : (slot + 1) * head] = act[
                    :, b * head : (b + 1) * head
                ]
        for b in range(2):
            peer = 2 * pair + b

            @pl.when(peer != c)
            def _(peer=peer):
                chain_copy(qkv_send.at[peer], qkv.at[mine], qkv_ss, qkv_rs, peer).start()

    qkv[mine, :] = qkv_send[c]

    pre = dot(normed_ref[...], wu[:, :width])
    sig = sigmoid(pre)
    gating_ref[...] = (pre * sig).astype(BF)
    pre_ref[:, :width] = sig * (1.0 + pre * (1.0 - sig))
    load_wo.wait()
    gated_grad = dot_nt(ct_ref[...], wo[...])
    gated_grad_ref[...] = gated_grad
    upstream = gated_grad * gating_ref[...].astype(F32)
    upstream = (upstream - mean(upstream)).astype(BF)
    for h in range(HEADS):
        h_send[h] = upstream[:, h * head : (h + 1) * head]
    for away in (4, 3, 5, 2, 6, 1, 7):
        peer = lax.rem(c + away, n_chain)
        chain_copy(h_send.at[peer], h_recv.at[mine], h_ss, h_rs, peer).start()
    h_recv[mine, :] = h_send[c]
    to_team(lambda other: ct_ref, ct_ref, ct_sems)

    def to_slope(step, carry):
        columns = pl.ds(pl.multiple_of(width + step * 512, 512), 512)
        v = pre_ref[:, columns]
        s = sigmoid(v)
        pre_ref[:, columns] = s * (1.0 + v * (1.0 - s))
        return carry

    lax.fori_loop(0, 3 * width // 512, to_slope, 0)

    def await_one(src, dst, send_sem, recv_sem, away):
        pltpu.make_async_remote_copy(
            src_ref=src,
            dst_ref=dst,
            send_sem=send_sem.at[away],
            recv_sem=recv_sem.at[away],
            device_id=(e, c),
            device_id_type=MESH,
        ).wait_recv()

    def await_chain(src, dst, send_sem, recv_sem):
        for away in range(1, n_chain):
            await_one(src, dst, send_sem, recv_sem, away)

    def await_sent(src, dst, send_sem, recv_sem):
        for away in range(1, n_chain):
            pltpu.make_async_remote_copy(
                src_ref=src,
                dst_ref=dst,
                send_sem=send_sem.at[away],
                recv_sem=recv_sem.at[away],
                device_id=(e, c),
                device_id_type=MESH,
            ).wait_send()

    await_chain(qkv_send.at[0], qkv.at[pl.ds(0, rows)], qkv_ss, qkv_rs)

    tile = 2 * rows
    tiles = tokens // tile
    key_t[...] = qkv[:, head : 2 * head].T
    value_t[...] = qkv[:, 2 * head :].T
    upper = iota((tile, tile), 0) <= iota((tile, tile), 1)
    for i in range(tiles):
        at_i = slice(tile * i, tile * (i + 1))
        until = slice(0, tile * (i + 1))
        query_ids = hist_ref[:, at_i].astype(F32)
        for j in range(i + 1):
            at_j = slice(tile * j, tile * (j + 1))
            scores = dot_nt(qkv[at_j, head : 2 * head], qkv[at_i, :head]) * alpha
            ids = hist_col[at_j, :]
            visible = jnp.concatenate([ids, ids], axis=1) == query_ids
            if i == j:
                visible = visible & upper
            sig = sigmoid(scores)
            att[at_j, at_i] = jnp.where(visible, scores * sig, 0.0).astype(BF)
            slope[at_j, at_i] = jnp.where(
                visible, (alpha * sig) * (1.0 + scores * (1.0 - sig)), 0.0
            )
        mix_t[:, at_i] = dot(value_t[:, until], att[until, at_i])

    await_chain(h_send.at[0], h_recv.at[pl.ds(0, rows)], h_ss, h_rs)
    mixed = mix_t[...]
    upstream = h_recv[...].astype(F32).T
    own_mean = jnp.mean(mixed, axis=0, keepdims=True)
    center = mixed - own_mean
    half = tokens // 2
    stats = jnp.zeros((8, half), F32)
    line_no = iota((8, half), 0)
    for k, stat in enumerate(
        (
            own_mean,
            jnp.sum(center * center, axis=0, keepdims=True),
            jnp.sum(upstream, axis=0, keepdims=True),
            jnp.sum(upstream * center, axis=0, keepdims=True),
        )
    ):
        stats = jnp.where(line_no == k, stat[:, :half], stats)
        stats = jnp.where(line_no == 4 + k, stat[:, half:], stats)
    stat_send[...] = stats
    for away in (4, 3, 5, 2, 6, 1, 7):
        peer = lax.rem(c + away, n_chain)
        chain_copy(stat_send, stat_recv.at[c], stat_ss, stat_rs, peer).start()
    stat_recv[c] = stats

    for i in range(tiles):
        at_i = slice(tile * i, tile * (i + 1))
        mix_send[at_i, :] = mix_t[:, at_i].T.astype(BF)
    for away in (4, 3, 5, 2, 6, 1, 7):
        peer = lax.rem(c + away, n_chain)
        there = pl.ds(pl.multiple_of(peer * rows, rows), rows)
        chain_copy(mix_send.at[there], mix_recv.at[c], mix_ss, mix_rs, peer).start()
    mix_recv[c] = mix_send[mine, :]

    await_chain(stat_send, stat_recv.at[0], stat_ss, stat_rs)
    halves = []
    for k in range(2):
        means, squares, sums, products = (
            [stat_recv[h, 4 * k + n : 4 * k + n + 1, :] for h in range(HEADS)] for n in range(4)
        )
        middle = sum(means) / HEADS
        squares = sum(squares) + head * sum((m - middle) * (m - middle) for m in means)
        products = sum(products) + sum(u * (m - middle) for u, m in zip(sums, means))
        inverse = lax.rsqrt(squares / width + epsilon)
        tilt = inverse * inverse * inverse * (products / width)
        halves.append((middle, inverse, sum(sums) / width, tilt))
    middle, inverse, lift, tilt = (
        jnp.concatenate([halves[0][n], halves[1][n]], axis=1) for n in range(4)
    )
    mixed_grad = inverse * (upstream - lift) - tilt * (mix_t[...] - middle)
    mg_t[...] = mixed_grad.astype(BF)
    mg[...] = mixed_grad.T.astype(BF)

    for i in range(tiles - 1, -1, -1):
        at_i = slice(tile * i, tile * (i + 1))
        until = slice(0, tile * (i + 1))
        after = slice(tile * i, tokens)
        for j in range(i + 1):
            at_j = slice(tile * j, tile * (j + 1))
            grad = dot(qkv[at_j, 2 * head :], mg_t[:, at_i])
            sgrad[at_j, at_i] = (grad * slope[at_j, at_i]).astype(BF)
        query_grad = dot(key_t[:, until], sgrad[until, at_i]).T
        key_grad = dot(sgrad[at_i, after], qkv[after, :head])
        value_grad = dot(att[at_i, after], mg[after, :])
        grads = jnp.concatenate([query_grad, key_grad, value_grad], axis=1).astype(BF)
        for b in range(2):
            peer = 2 * i + b
            d_send[peer] = grads[rows * b : rows * (b + 1), :]

    def send_grads(*distances):
        for away in distances:
            peer = lax.rem(c + away, n_chain)
            chain_copy(d_send.at[peer], d_recv.at[c], d_ss, d_rs, peer).start()

    send_grads(1, 7, 2, 6)
    d_recv[c] = d_send[c]

    await_chain(mix_send.at[pl.ds(0, rows)], mix_recv.at[0], mix_ss, mix_rs)
    mixed = jnp.concatenate([mix_recv[h] for h in range(HEADS)], axis=1).astype(F32)
    center = mixed - mean(mixed)
    mixed_norm = center * lax.rsqrt(mean(center * center) + epsilon)
    gating = gating_ref[...].astype(F32)
    gated_grad = gated_grad_ref[...]
    gated_ref[...] = (mixed_norm * gating).astype(BF)
    pg_ref[:, :width] = (gated_grad * mixed_norm * pre_ref[:, :width]).astype(BF)

    for h in range(team):
        gt_send[h] = gated_ref[:, h * rows : (h + 1) * rows]
    own_gt = pl.ds(pl.multiple_of(seat * rows, rows), rows)
    to_team(lambda other: gt_send.at[other], gt_recv.at[own_gt], gt_sems)
    gt_recv[own_gt, :] = gt_send[seat]
    send_grads(3, 5)

    layer_out_ref[...] = (residual_ref[...] + dot(gated_ref[...], wo[...])).astype(BF)
    store_lo = pltpu.make_async_copy(layer_out_ref, layer_out_hbm, store_sem.at[0])
    store_lo.start()
    ng_ref[...] = dot_nt(pg_ref[:, :width], wu[:, :width])

    await_group(ct_all, ct_sems.at[1], rows, team - 1)
    await_group(gt_recv, gt_sems.at[1], rows, team - 1)
    grad_scale = 1.0 / math.sqrt(rows * n_dp * n_chain)
    term = (dot_tn(gt_recv[...], ct_all[...]) * grad_scale).astype(BF)
    line = e // team

    def wg_copy(k, owner):
        return pltpu.make_async_remote_copy(
            src_ref=wg_send.at[k],
            dst_ref=wg_recv.at[line],
            send_sem=wg_ss.at[k],
            recv_sem=wg_rs.at[line],
            device_id=(owner, c),
            device_id_type=MESH,
        )

    for k in range(teams):
        wg_send[k] = term[k * share : (k + 1) * share, :]
        owner = seat * teams + k

        @pl.when(owner != e)
        def _(k=k, owner=owner):
            wg_copy(k, owner).start()

        @pl.when(owner == e)
        def _(k=k):
            wg_recv[line] = wg_send[k]

    send_grads(4)

    summed = None
    for k in range(teams):
        @pl.when(k * team + e // teams != e)
        def _(k=k):
            pltpu.make_async_copy(wg_recv.at[k], wg_recv.at[k], wg_rs.at[k]).wait()

    for k in range(teams):
        part = wg_recv[k].astype(F32)
        summed = part if summed is None else summed + part
    summed = summed.astype(BF)
    for h in range(n_chain):
        part_send[h] = summed[:, h * head : (h + 1) * head]
    for away in (4, 3, 5, 2, 6, 1, 7):
        peer = lax.rem(c + away, n_chain)
        chain_copy(part_send.at[peer], part_recv.at[c], part_ss, part_rs, peer).start()
    part_recv[c] = part_send[c]

    residual = residual_ref[...]
    center = residual - mean(residual)
    inverse = lax.rsqrt(mean(center * center) + epsilon)
    residual_ref[...] = center * inverse
    inverse_ref[...] = jnp.broadcast_to(inverse, (rows, rows))
    slot_col = ev_recv[:, cols : cols + rows].astype(F32).astype(I32)
    slot_there = slot_col == iota((total, rows), 1)
    quarter = lax.rem(iota((total, rows), 0), block) // per_peer
    for q in range(fold):
        back_ref[:, q * rows : (q + 1) * rows] = one_hot(slot_there & (quarter == q))
    place = jnp.concatenate([place_col] * fold, axis=1)
    here = iota((rows, total), 1)
    for q in range(fold):
        home_ref[q] = one_hot(here == place + per_peer * q)

    for pair in ((0, 1), (7, 2), (6, 3), (5, 4)):
        for away in pair:
            if away:
                await_one(d_send.at[0], d_recv.at[0], d_ss, d_rs, away)
        froms = [lax.rem(c - away + n_chain, n_chain) for away in pair]
        terms = []
        for slot, part in ((0, 2), (1, 3), (2, 1)):
            spans = [
                pl.ds(pl.multiple_of(part * width + h * head, head), head) for h in froms
            ]
            grads = [
                (
                    d_recv[h, :, slot * head : (slot + 1) * head].astype(F32)
                    * pre_ref[:, span]
                ).astype(BF)
                for h, span in zip(froms, spans)
            ]
            terms.append(
                dot_nt(
                    jnp.concatenate(grads, axis=1),
                    jnp.concatenate([wu[:, span] for span in spans], axis=1),
                )
            )
        ng_ref[...] += terms[0] + terms[1] + terms[2]
    normed_grad = ng_ref[...]
    normed = residual_ref[...]
    input_grad = ct_ref[...].astype(F32) + inverse_ref[:, :1] * (
        normed_grad - mean(normed_grad) - normed * mean(normed_grad * normed)
    )
    input_grad = input_grad.astype(BF)

    stacked = jnp.concatenate(
        [input_grad[:, cols * q : cols * (q + 1)] for q in range(fold)], axis=0
    )
    ret_send[...] = dot(back_ref[...], stacked).astype(BF)
    ret_recv[own_ev, :] = ret_send[own_ev, :]
    lax.fori_loop(1, n_dp, to_group(ret_send, ret_recv, ret_sems, block), 0)

    await_chain(part_send.at[0], part_recv.at[0], part_ss, part_rs)
    whole = part_recv[0].astype(F32)
    for h in range(1, n_chain):
        whole = whole + part_recv[h].astype(F32)
    full_send[...] = whole.astype(BF)
    for away in (4, 3, 5, 2, 6, 1, 7):
        peer = lax.rem(c + away, n_chain)
        chain_copy(full_send, full_recv.at[c], full_ss, full_rs, peer).start()
    full_recv[c] = full_send[...]

    await_group(ret_recv, ret_sems.at[1], block)
    returned = ret_recv[...]
    for q in range(fold):
        event_grad_ref[:, cols * q : cols * (q + 1)] = dot(home_ref[q], returned).astype(BF)

    await_chain(full_send, full_recv.at[0], full_ss, full_rs)
    for h in range(n_chain):
        weight_grad_ref[:, h * head : (h + 1) * head] = full_recv[h].astype(F32)
    store_wg = pltpu.make_async_copy(weight_grad_ref, weight_grad_hbm, store_sem.at[1])
    store_wg.start()

    await_group(ev_send, ev_sems.at[0], block)
    await_group(ct_all, ct_sems.at[0], rows, team - 1)
    await_group(gt_recv, gt_sems.at[0], rows, team - 1)
    for k in range(teams):
        @pl.when(seat * teams + k != e)
        def _(k=k):
            pltpu.make_async_copy(wg_send.at[k], wg_send.at[k], wg_ss.at[k]).wait()

    await_group(ret_send, ret_sems.at[0], block)
    await_sent(qkv_send.at[0], qkv.at[pl.ds(0, rows)], qkv_ss, qkv_rs)
    await_sent(mix_send.at[pl.ds(0, rows)], mix_recv.at[0], mix_ss, mix_rs)
    await_sent(h_send.at[0], h_recv.at[pl.ds(0, rows)], h_ss, h_rs)
    await_sent(stat_send, stat_recv.at[0], stat_ss, stat_rs)
    await_sent(d_send.at[0], d_recv.at[0], d_ss, d_rs)
    await_sent(part_send.at[0], part_recv.at[0], part_ss, part_rs)
    await_sent(full_send, full_recv.at[0], full_ss, full_rs)
    store_lo.wait()
    store_wg.wait()


def hand_over(a, b, c, a_out, b_out, c_out):
    a_out[...] = a[...]
    b_out[...] = b[...]
    c_out[...] = c[...]


def on_device(n_dp, n_chain, events, destinations, history_ids, cotangent, w_uvqk, w_out):
    _, rows, width = events.shape
    head = width // HEADS
    tokens = rows * n_chain
    per_peer = rows // n_dp
    fold = max(1, 16 // per_peer)
    total = rows * fold
    cols = width // fold
    share = width // n_dp
    vmem = pl.BlockSpec(memory_space=pltpu.VMEM)
    anywhere = pl.BlockSpec(memory_space=pl.ANY)
    pair = pltpu.SemaphoreType.DMA((2,))
    quad = pltpu.SemaphoreType.DMA((rows // share,))
    ring = pltpu.SemaphoreType.DMA((n_chain,))
    results = pl.pallas_call(
        functools.partial(kernel, n_dp, n_chain),
        out_shape=(
            jax.ShapeDtypeStruct((rows, width), BF),
            jax.ShapeDtypeStruct((rows, width), BF),
            jax.ShapeDtypeStruct((share, width), F32),
        ),
        in_specs=[vmem, vmem, anywhere, anywhere, anywhere, anywhere],
        out_specs=(vmem, anywhere, anywhere),
        scratch_shapes=[
            pltpu.VMEM((rows, width), BF),
            pltpu.VMEM((width, width), BF),
            pltpu.VMEM((rows, width), BF),
            pltpu.VMEM((share, width), F32),
            pltpu.VMEM((width, 4 * width), BF),
            pltpu.VMEM((width, width), BF),
            pltpu.VMEM((total, cols + rows), BF),
            pltpu.VMEM((total, cols + rows), BF),
            pltpu.VMEM((rows, width), F32),
            pltpu.VMEM((rows, width), BF),
            pltpu.VMEM((rows, 4 * width), F32),
            pltpu.VMEM((rows, width), BF),
            pltpu.VMEM((rows, width), F32),
            pltpu.VMEM((n_chain, rows, 3 * head), BF),
            pltpu.VMEM((tokens, 3 * head), BF),
            pltpu.VMEM((tokens, rows), F32),
            pltpu.VMEM((tokens, tokens), BF),
            pltpu.VMEM((tokens, tokens), F32),
            pltpu.VMEM((tokens, tokens), BF),
            pltpu.VMEM((tokens, head), BF),
            pltpu.VMEM((n_chain, rows, head), BF),
            pltpu.VMEM((n_chain, rows, head), BF),
            pltpu.VMEM((tokens, head), BF),
            pltpu.VMEM((8, tokens // 2), F32),
            pltpu.VMEM((n_chain, 8, tokens // 2), F32),
            pltpu.VMEM((head, tokens), F32),
            pltpu.VMEM((head, tokens), BF),
            pltpu.VMEM((head, tokens), BF),
            pltpu.VMEM((head, tokens), BF),
            pltpu.VMEM((tokens, head), BF),
            pltpu.VMEM((rows, width), BF),
            pltpu.VMEM((width // rows, rows, rows), BF),
            pltpu.VMEM((width, rows), BF),
            pltpu.VMEM((rows // share, share, width), BF),
            pltpu.VMEM((rows // share, share, width), BF),
            pltpu.VMEM((n_chain, rows, 3 * head), BF),
            pltpu.VMEM((n_chain, rows, 3 * head), BF),
            pltpu.VMEM((rows, 4 * width), BF),
            pltpu.VMEM((rows, width), F32),
            pltpu.VMEM((n_chain, share, head), BF),
            pltpu.VMEM((n_chain, share, head), BF),
            pltpu.VMEM((share, head), BF),
            pltpu.VMEM((n_chain, share, head), BF),
            pltpu.VMEM((total, total), BF),
            pltpu.VMEM((fold, rows, total), BF),
            pltpu.VMEM((rows, rows), F32),
            pltpu.VMEM((total, cols), BF),
            pltpu.VMEM((total, cols), BF),
            pltpu.SemaphoreType.DMA((4,)),
            pair,
            pair,
            pair,
            pair,
            quad,
            quad,
            pair,
        ]
        + [ring] * 14,
        compiler_params=pltpu.CompilerParams(
            collective_id=0, has_side_effects=True, vmem_limit_bytes=56 * 1024 * 1024
        ),
        cost_estimate=pl.CostEstimate(
            flops=9 * 2**30, bytes_accessed=12 * 2**20, transcendentals=4 * 2**20
        ),
        name="hstu_layer",
    )(destinations, history_ids, events[0], cotangent[0], w_uvqk, w_out)
    event_grad, layer_out, weight_grad = pl.pallas_call(
        hand_over,
        out_shape=tuple(jax.ShapeDtypeStruct(r.shape, r.dtype) for r in results),
        in_specs=[vmem] * 3,
        out_specs=(vmem,) * 3,
        name="hand_over",
    )(*results)
    return (layer_out[None], event_grad[None], weight_grad)


def solution(mesh):
    return jax.shard_map(
        functools.partial(on_device, mesh.shape["dp"], mesh.shape["chain"]),
        mesh=mesh,
        in_specs=(
            P("dp", "chain", None),
            P("dp", "chain"),
            P("dp", None),
            P("dp", "chain", None),
            P(),
            P(),
        ),
        out_specs=(P("dp", "chain", None), P("dp", "chain", None), P("dp", None)),
        check_vma=False,
    )
```

```python
import functools
import math

import jax
import jax.numpy as jnp
from jax import lax
from jax.experimental import pallas as pl
from jax.experimental.pallas import tpu as pltpu
from jax.sharding import PartitionSpec as P

HEADS = 8
MESH = pl.DeviceIdType.MESH
BF = jnp.bfloat16
F32 = jnp.float32
I32 = jnp.int32
epsilon = 1e-05


def dot(a, b):
    return lax.dot_general(a, b, (((1,), (0,)), ((), ())), preferred_element_type=F32)


def dot_nt(a, b):
    return lax.dot_general(a, b, (((1,), (1,)), ((), ())), preferred_element_type=F32)


def dot_tn(a, b):
    return lax.dot_general(a, b, (((0,), (0,)), ((), ())), preferred_element_type=F32)


def sigmoid(v):
    return 0.5 * jnp.tanh(0.5 * v) + 0.5


def iota(shape, dim):
    return lax.broadcasted_iota(I32, shape, dim)


def mean(v):
    return jnp.mean(v, axis=-1, keepdims=True)


def one_hot(mask):
    return jnp.where(mask, 1.0, 0.0).astype(BF)


def kernel(
    n_dp,
    n_chain,
    dest_hbm,
    hist_hbm,
    ev_hbm,
    ct_hbm,
    wu_hbm,
    wo_hbm,
    event_grad_hbm,
    layer_out_hbm,
    weight_grad_hbm,
    dest_ref,
    hist_ref,
    ev_ref,
    ct_all,
    event_grad_ref,
    layer_out_ref,
    weight_grad_ref,
    wu,
    wo,
    ev_send,
    ev_recv,
    residual_ref,
    normed_ref,
    pre_ref,
    gating_ref,
    gated_grad_ref,
    qkv_send,
    qkv,
    hist_col,
    att,
    slope,
    sgrad,
    mix_send,
    mix_recv,
    h_send,
    h_recv,
    stat_send,
    stat_recv,
    mix_t,
    key_t,
    value_t,
    mg_t,
    mg,
    gated_ref,
    gt_send,
    gt_recv,
    wg_send,
    wg_recv,
    d_send,
    d_recv,
    pg_ref,
    ng_ref,
    part_send,
    part_recv,
    full_send,
    full_recv,
    back_ref,
    home_ref,
    inverse_ref,
    ret_send,
    ret_recv,
    load_sem,
    store_sem,
    ev_sems,
    ct_sems,
    gt_sems,
    wg_ss,
    wg_rs,
    ret_sems,
    qkv_ss,
    qkv_rs,
    mix_ss,
    mix_rs,
    h_ss,
    h_rs,
    stat_ss,
    stat_rs,
    d_ss,
    d_rs,
    part_ss,
    part_rs,
    full_ss,
    full_rs,
):
    rows, width = ev_ref.shape
    head = width // HEADS
    tokens = rows * n_chain
    per_peer = rows // n_dp
    fold = max(1, 16 // per_peer)
    block = per_peer * fold
    total = rows * fold
    cols = width // fold
    alpha = head ** (-0.5)
    share = width // n_dp
    e = lax.axis_index("dp")
    c = lax.axis_index("chain")
    team = width // rows
    teams = n_dp // team
    seat = lax.rem(e, team)
    ct_ref = ct_all.at[pl.ds(pl.multiple_of(seat * rows, rows), rows)]

    load_ev = pltpu.make_async_copy(ev_hbm, ev_ref, load_sem.at[2])
    load_ct = pltpu.make_async_copy(ct_hbm, ct_ref, load_sem.at[3])
    load_wu = pltpu.make_async_copy(wu_hbm, wu, load_sem.at[0])
    load_wo = pltpu.make_async_copy(wo_hbm, wo, load_sem.at[1])
    load_dest = pltpu.make_async_copy(dest_hbm, dest_ref, load_sem.at[4])
    load_hist = pltpu.make_async_copy(hist_hbm, hist_ref, load_sem.at[5])
    load_dest.start()
    load_ev.start()
    load_hist.start()

    barrier = pltpu.get_barrier_semaphore()

    def greet(step, carry):
        pl.semaphore_signal(
            barrier, inc=1, device_id=(lax.rem(e + step, n_dp), c), device_id_type=MESH
        )
        return carry

    lax.fori_loop(1, n_dp, greet, 0)
    for step in range(1, n_chain):
        pl.semaphore_signal(
            barrier, inc=1, device_id=(e, lax.rem(c + step, n_chain)), device_id_type=MESH
        )

    load_wu.start()
    load_ct.start()
    load_wo.start()

    ri = iota((rows, rows), 0)
    ci = iota((rows, rows), 1)
    eye = ri == ci
    load_dest.wait()
    d_row = jnp.broadcast_to(dest_ref[...], (rows, rows))
    d_col = jnp.sum(jnp.where(eye, d_row.astype(F32), 0.0), axis=1, keepdims=True)
    d_col = jnp.broadcast_to(d_col, (rows, rows)).astype(I32)
    t_row = d_row // rows
    t_col = d_col // rows
    same = t_row == t_col
    rank_row = jnp.sum(jnp.where(same & (ri < ci), 1.0, 0.0), axis=0, keepdims=True)
    rank_col = jnp.sum(jnp.where(same & (ci < ri), 1.0, 0.0), axis=1, keepdims=True)
    place_row = block * t_row[:1, :] + rank_row.astype(I32)
    place_col = block * t_col + jnp.broadcast_to(rank_col, (rows, rows)).astype(I32)
    slots = (d_col - t_col * rows).astype(F32).astype(BF)
    at_row = jnp.broadcast_to(place_row, (total, rows))
    at = iota((total, rows), 0)
    spread = jnp.concatenate(
        [one_hot(at == at_row + per_peer * q) for q in range(fold)], axis=1
    )
    load_ev.wait()
    packed = jnp.concatenate(
        [
            jnp.concatenate([ev_ref[:, cols * q : cols * (q + 1)], slots], axis=1)
            for q in range(fold)
        ],
        axis=0,
    )
    ev_send[...] = dot(spread, packed).astype(BF)
    own_ev = pl.ds(pl.multiple_of(e * block, block), block)
    ev_recv[own_ev, :] = ev_send[own_ev, :]

    pl.semaphore_wait(barrier, n_dp - 1 + n_chain - 1)

    def to_group(send, recv, sems, rows_each):
        here = pl.ds(pl.multiple_of(e * rows_each, rows_each), rows_each)

        def one(step, carry):
            peer = lax.rem(e + step, n_dp)
            there = pl.ds(pl.multiple_of(peer * rows_each, rows_each), rows_each)
            pltpu.make_async_remote_copy(
                src_ref=send.at[there],
                dst_ref=recv.at[here],
                send_sem=sems.at[0],
                recv_sem=sems.at[1],
                device_id=(peer, c),
                device_id_type=MESH,
            ).start()
            return carry

        return one

    def await_group(buffer, sem, rows_each, peers=n_dp - 1):
        part = buffer.at[pl.ds(0, peers * rows_each)]
        pltpu.make_async_copy(part, part, sem).wait()

    lax.fori_loop(1, n_dp, to_group(ev_send, ev_recv, ev_sems, block), 0)

    load_hist.wait()
    for b in range(n_chain):
        ids = jnp.broadcast_to(
            hist_ref[:, rows * b : rows * (b + 1)].astype(F32), (rows, rows)
        )
        hist_col[rows * b : rows * (b + 1), :] = jnp.broadcast_to(
            jnp.sum(jnp.where(eye, ids, 0.0), axis=1, keepdims=True), (rows, rows)
        )

    def to_team(src, dst, sems):
        for step in range(1, team):
            other = lax.rem(seat + step, team)
            pltpu.make_async_remote_copy(
                src_ref=src(other),
                dst_ref=dst,
                send_sem=sems.at[0],
                recv_sem=sems.at[1],
                device_id=(e - seat + other, c),
                device_id_type=MESH,
            ).start()

    await_group(ev_recv, ev_sems.at[1], block)
    load_ct.wait()
    slot_col = ev_recv[:, cols : cols + rows].astype(F32).astype(I32)
    slot_row = jnp.concatenate(
        [
            jnp.sum(
                jnp.where(eye, slot_col[rows * b : rows * (b + 1), :], 0).astype(F32),
                axis=0,
                keepdims=True,
            )
            for b in range(fold)
        ],
        axis=1,
    ).astype(I32)
    slot_row = jnp.broadcast_to(slot_row, (rows, total))
    slot_here = slot_row == iota((rows, total), 0)
    quarter = lax.rem(iota((rows, total), 1), block) // per_peer
    arrived = ev_recv[:, :cols]
    residual = jnp.concatenate(
        [dot(one_hot(slot_here & (quarter == q)), arrived) for q in range(fold)], axis=1
    )
    residual_ref[...] = residual
    center = residual - mean(residual)
    inverse = lax.rsqrt(mean(center * center) + epsilon)
    normed_ref[...] = (center * inverse).astype(BF)

    def chain_copy(src, dst, send_sem, recv_sem, peer):
        away = lax.rem(peer - c + n_chain, n_chain)
        return pltpu.make_async_remote_copy(
            src_ref=src,
            dst_ref=dst,
            send_sem=send_sem.at[away],
            recv_sem=recv_sem.at[away],
            device_id=(e, peer),
            device_id_type=MESH,
        )

    mine = pl.ds(pl.multiple_of(c * rows, rows), rows)

    load_wu.wait()
    for turn in (2, 1, 3, 0):
        pair = lax.rem(c // 2 + turn, n_chain // 2)
        for slot, part in ((0, 2), (1, 3), (2, 1)):
            columns = pl.ds(pl.multiple_of(part * width + pair * 2 * head, 2 * head), 2 * head)
            pre = dot(normed_ref[...], wu[:, columns])
            pre_ref[:, columns] = pre
            act = (pre * sigmoid(pre)).astype(BF)
            for b in range(2):
                qkv_send[2 * pair + b, :, slot * head : (slot + 1) * head] = act[
                    :, b * head : (b + 1) * head
                ]
        for b in range(2):
            peer = 2 * pair + b

            @pl.when(peer != c)
            def _(peer=peer):
                chain_copy(qkv_send.at[peer], qkv.at[mine], qkv_ss, qkv_rs, peer).start()

    qkv[mine, :] = qkv_send[c]

    pre = dot(normed_ref[...], wu[:, :width])
    sig = sigmoid(pre)
    gating_ref[...] = (pre * sig).astype(BF)
    pre_ref[:, :width] = sig * (1.0 + pre * (1.0 - sig))
    load_wo.wait()
    gated_grad = dot_nt(ct_ref[...], wo[...])
    gated_grad_ref[...] = gated_grad
    upstream = gated_grad * gating_ref[...].astype(F32)
    upstream = (upstream - mean(upstream)).astype(BF)
    for h in range(HEADS):
        h_send[h] = upstream[:, h * head : (h + 1) * head]
    for away in (4, 3, 5, 2, 6, 1, 7):
        peer = lax.rem(c + away, n_chain)
        chain_copy(h_send.at[peer], h_recv.at[mine], h_ss, h_rs, peer).start()
    h_recv[mine, :] = h_send[c]
    to_team(lambda other: ct_ref, ct_ref, ct_sems)

    def to_slope(step, carry):
        columns = pl.ds(pl.multiple_of(width + step * 512, 512), 512)
        v = pre_ref[:, columns]
        s = sigmoid(v)
        pre_ref[:, columns] = s * (1.0 + v * (1.0 - s))
        return carry

    lax.fori_loop(0, 3 * width // 512, to_slope, 0)

    def await_one(src, dst, send_sem, recv_sem, away):
        pltpu.make_async_remote_copy(
            src_ref=src,
            dst_ref=dst,
            send_sem=send_sem.at[away],
            recv_sem=recv_sem.at[away],
            device_id=(e, c),
            device_id_type=MESH,
        ).wait_recv()

    def await_chain(src, dst, send_sem, recv_sem):
        for away in range(1, n_chain):
            await_one(src, dst, send_sem, recv_sem, away)

    def await_sent(src, dst, send_sem, recv_sem):
        for away in range(1, n_chain):
            pltpu.make_async_remote_copy(
                src_ref=src,
                dst_ref=dst,
                send_sem=send_sem.at[away],
                recv_sem=recv_sem.at[away],
                device_id=(e, c),
                device_id_type=MESH,
            ).wait_send()

    await_chain(qkv_send.at[0], qkv.at[pl.ds(0, rows)], qkv_ss, qkv_rs)

    tile = 2 * rows
    tiles = tokens // tile
    key_t[...] = qkv[:, head : 2 * head].T
    value_t[...] = qkv[:, 2 * head :].T
    upper = iota((tile, tile), 0) <= iota((tile, tile), 1)
    for i in range(tiles):
        at_i = slice(tile * i, tile * (i + 1))
        until = slice(0, tile * (i + 1))
        query_ids = hist_ref[:, at_i].astype(F32)
        for j in range(i + 1):
            at_j = slice(tile * j, tile * (j + 1))
            scores = dot_nt(qkv[at_j, head : 2 * head], qkv[at_i, :head]) * alpha
            ids = hist_col[at_j, :]
            visible = jnp.concatenate([ids, ids], axis=1) == query_ids
            if i == j:
                visible = visible & upper
            sig = sigmoid(scores)
            att[at_j, at_i] = jnp.where(visible, scores * sig, 0.0).astype(BF)
            slope[at_j, at_i] = jnp.where(
                visible, (alpha * sig) * (1.0 + scores * (1.0 - sig)), 0.0
            )
        mix_t[:, at_i] = dot(value_t[:, until], att[until, at_i])

    await_chain(h_send.at[0], h_recv.at[pl.ds(0, rows)], h_ss, h_rs)
    mixed = mix_t[...]
    upstream = h_recv[...].astype(F32).T
    own_mean = jnp.mean(mixed, axis=0, keepdims=True)
    center = mixed - own_mean
    half = tokens // 2
    stats = jnp.zeros((8, half), F32)
    line_no = iota((8, half), 0)
    for k, stat in enumerate(
        (
            own_mean,
            jnp.sum(center * center, axis=0, keepdims=True),
            jnp.sum(upstream, axis=0, keepdims=True),
            jnp.sum(upstream * center, axis=0, keepdims=True),
        )
    ):
        stats = jnp.where(line_no == k, stat[:, :half], stats)
        stats = jnp.where(line_no == 4 + k, stat[:, half:], stats)
    stat_send[...] = stats
    for away in (4, 3, 5, 2, 6, 1, 7):
        peer = lax.rem(c + away, n_chain)
        chain_copy(stat_send, stat_recv.at[c], stat_ss, stat_rs, peer).start()
    stat_recv[c] = stats

    for i in range(tiles):
        at_i = slice(tile * i, tile * (i + 1))
        mix_send[at_i, :] = mix_t[:, at_i].T.astype(BF)
    for away in (4, 3, 5, 2, 6, 1, 7):
        peer = lax.rem(c + away, n_chain)
        there = pl.ds(pl.multiple_of(peer * rows, rows), rows)
        chain_copy(mix_send.at[there], mix_recv.at[c], mix_ss, mix_rs, peer).start()
    mix_recv[c] = mix_send[mine, :]

    await_chain(stat_send, stat_recv.at[0], stat_ss, stat_rs)
    halves = []
    for k in range(2):
        means, squares, sums, products = (
            [stat_recv[h, 4 * k + n : 4 * k + n + 1, :] for h in range(HEADS)] for n in range(4)
        )
        middle = sum(means) / HEADS
        squares = sum(squares) + head * sum((m - middle) * (m - middle) for m in means)
        products = sum(products) + sum(u * (m - middle) for u, m in zip(sums, means))
        inverse = lax.rsqrt(squares / width + epsilon)
        tilt = inverse * inverse * inverse * (products / width)
        halves.append((middle, inverse, sum(sums) / width, tilt))
    middle, inverse, lift, tilt = (
        jnp.concatenate([halves[0][n], halves[1][n]], axis=1) for n in range(4)
    )
    mixed_grad = inverse * (upstream - lift) - tilt * (mix_t[...] - middle)
    mg_t[...] = mixed_grad.astype(BF)
    mg[...] = mixed_grad.T.astype(BF)

    for i in range(tiles - 1, -1, -1):
        at_i = slice(tile * i, tile * (i + 1))
        until = slice(0, tile * (i + 1))
        after = slice(tile * i, tokens)
        for j in range(i + 1):
            at_j = slice(tile * j, tile * (j + 1))
            grad = dot(qkv[at_j, 2 * head :], mg_t[:, at_i])
            sgrad[at_j, at_i] = (grad * slope[at_j, at_i]).astype(BF)
        query_grad = dot(key_t[:, until], sgrad[until, at_i]).T
        key_grad = dot(sgrad[at_i, after], qkv[after, :head])
        value_grad = dot(att[at_i, after], mg[after, :])
        grads = jnp.concatenate([query_grad, key_grad, value_grad], axis=1).astype(BF)
        for b in range(2):
            peer = 2 * i + b
            d_send[peer] = grads[rows * b : rows * (b + 1), :]

    def send_grads(*distances):
        for away in distances:
            peer = lax.rem(c + away, n_chain)
            chain_copy(d_send.at[peer], d_recv.at[c], d_ss, d_rs, peer).start()

    send_grads(1, 7, 2, 6)
    d_recv[c] = d_send[c]

    await_chain(mix_send.at[pl.ds(0, rows)], mix_recv.at[0], mix_ss, mix_rs)
    mixed = jnp.concatenate([mix_recv[h] for h in range(HEADS)], axis=1).astype(F32)
    center = mixed - mean(mixed)
    mixed_norm = center * lax.rsqrt(mean(center * center) + epsilon)
    gating = gating_ref[...].astype(F32)
    gated_grad = gated_grad_ref[...]
    gated_ref[...] = (mixed_norm * gating).astype(BF)
    pg_ref[:, :width] = (gated_grad * mixed_norm * pre_ref[:, :width]).astype(BF)

    for h in range(team):
        gt_send[h] = gated_ref[:, h * rows : (h + 1) * rows]
    own_gt = pl.ds(pl.multiple_of(seat * rows, rows), rows)
    to_team(lambda other: gt_send.at[other], gt_recv.at[own_gt], gt_sems)
    gt_recv[own_gt, :] = gt_send[seat]
    send_grads(3, 5)

    layer_out_ref[...] = (residual_ref[...] + dot(gated_ref[...], wo[...])).astype(BF)
    store_lo = pltpu.make_async_copy(layer_out_ref, layer_out_hbm, store_sem.at[0])
    store_lo.start()
    ng_ref[...] = dot_nt(pg_ref[:, :width], wu[:, :width])

    await_group(ct_all, ct_sems.at[1], rows, team - 1)
    await_group(gt_recv, gt_sems.at[1], rows, team - 1)
    grad_scale = 1.0 / math.sqrt(rows * n_dp * n_chain)
    term = (dot_tn(gt_recv[...], ct_all[...]) * grad_scale).astype(BF)
    line = e // team

    def wg_copy(k, owner):
        return pltpu.make_async_remote_copy(
            src_ref=wg_send.at[k],
            dst_ref=wg_recv.at[line],
            send_sem=wg_ss.at[k],
            recv_sem=wg_rs.at[line],
            device_id=(owner, c),
            device_id_type=MESH,
        )

    for k in range(teams):
        wg_send[k] = term[k * share : (k + 1) * share, :]
        owner = seat * teams + k

        @pl.when(owner != e)
        def _(k=k, owner=owner):
            wg_copy(k, owner).start()

        @pl.when(owner == e)
        def _(k=k):
            wg_recv[line] = wg_send[k]

    send_grads(4)

    summed = None
    for k in range(teams):
        @pl.when(k * team + e // teams != e)
        def _(k=k):
            pltpu.make_async_copy(wg_recv.at[k], wg_recv.at[k], wg_rs.at[k]).wait()

    for k in range(teams):
        part = wg_recv[k].astype(F32)
        summed = part if summed is None else summed + part
    summed = summed.astype(BF)
    for h in range(n_chain):
        part_send[h] = summed[:, h * head : (h + 1) * head]
    for away in (4, 3, 5, 2, 6, 1, 7):
        peer = lax.rem(c + away, n_chain)
        chain_copy(part_send.at[peer], part_recv.at[c], part_ss, part_rs, peer).start()
    part_recv[c] = part_send[c]

    residual = residual_ref[...]
    center = residual - mean(residual)
    inverse = lax.rsqrt(mean(center * center) + epsilon)
    residual_ref[...] = center * inverse
    inverse_ref[...] = jnp.broadcast_to(inverse, (rows, rows))
    slot_col = ev_recv[:, cols : cols + rows].astype(F32).astype(I32)
    slot_there = slot_col == iota((total, rows), 1)
    quarter = lax.rem(iota((total, rows), 0), block) // per_peer
    for q in range(fold):
        back_ref[:, q * rows : (q + 1) * rows] = one_hot(slot_there & (quarter == q))
    place = jnp.concatenate([place_col] * fold, axis=1)
    here = iota((rows, total), 1)
    for q in range(fold):
        home_ref[q] = one_hot(here == place + per_peer * q)

    for pair in ((0, 1), (7, 2), (6, 3), (5, 4)):
        for away in pair:
            if away:
                await_one(d_send.at[0], d_recv.at[0], d_ss, d_rs, away)
        froms = [lax.rem(c - away + n_chain, n_chain) for away in pair]
        terms = []
        for slot, part in ((0, 2), (1, 3), (2, 1)):
            spans = [
                pl.ds(pl.multiple_of(part * width + h * head, head), head) for h in froms
            ]
            grads = [
                (
                    d_recv[h, :, slot * head : (slot + 1) * head].astype(F32)
                    * pre_ref[:, span]
                ).astype(BF)
                for h, span in zip(froms, spans)
            ]
            terms.append(
                dot_nt(
                    jnp.concatenate(grads, axis=1),
                    jnp.concatenate([wu[:, span] for span in spans], axis=1),
                )
            )
        ng_ref[...] += terms[0] + terms[1] + terms[2]
    normed_grad = ng_ref[...]
    normed = residual_ref[...]
    input_grad = ct_ref[...].astype(F32) + inverse_ref[:, :1] * (
        normed_grad - mean(normed_grad) - normed * mean(normed_grad * normed)
    )
    input_grad = input_grad.astype(BF)

    stacked = jnp.concatenate(
        [input_grad[:, cols * q : cols * (q + 1)] for q in range(fold)], axis=0
    )
    ret_send[...] = dot(back_ref[...], stacked).astype(BF)
    ret_recv[own_ev, :] = ret_send[own_ev, :]
    lax.fori_loop(1, n_dp, to_group(ret_send, ret_recv, ret_sems, block), 0)

    await_chain(part_send.at[0], part_recv.at[0], part_ss, part_rs)
    whole = part_recv[0].astype(F32)
    for h in range(1, n_chain):
        whole = whole + part_recv[h].astype(F32)
    full_send[...] = whole.astype(BF)
    for away in (4, 3, 5, 2, 6, 1, 7):
        peer = lax.rem(c + away, n_chain)
        chain_copy(full_send, full_recv.at[c], full_ss, full_rs, peer).start()
    full_recv[c] = full_send[...]

    await_group(ev_send, ev_sems.at[0], block)
    await_group(ct_all, ct_sems.at[0], rows, team - 1)
    await_group(gt_recv, gt_sems.at[0], rows, team - 1)
    for k in range(teams):
        @pl.when(seat * teams + k != e)
        def _(k=k):
            pltpu.make_async_copy(wg_send.at[k], wg_send.at[k], wg_ss.at[k]).wait()

    await_sent(qkv_send.at[0], qkv.at[pl.ds(0, rows)], qkv_ss, qkv_rs)
    await_sent(mix_send.at[pl.ds(0, rows)], mix_recv.at[0], mix_ss, mix_rs)
    await_sent(h_send.at[0], h_recv.at[pl.ds(0, rows)], h_ss, h_rs)
    await_sent(stat_send, stat_recv.at[0], stat_ss, stat_rs)
    await_sent(d_send.at[0], d_recv.at[0], d_ss, d_rs)
    await_sent(part_send.at[0], part_recv.at[0], part_ss, part_rs)
    store_lo.wait()

    await_group(ret_recv, ret_sems.at[1], block)
    returned = ret_recv[...]
    for q in range(fold):
        event_grad_ref[:, cols * q : cols * (q + 1)] = dot(home_ref[q], returned).astype(BF)
    store_eg = pltpu.make_async_copy(event_grad_ref, event_grad_hbm, store_sem.at[2])
    store_eg.start()

    await_chain(full_send, full_recv.at[0], full_ss, full_rs)
    for h in range(n_chain):
        weight_grad_ref[:, h * head : (h + 1) * head] = full_recv[h].astype(F32)
    store_wg = pltpu.make_async_copy(weight_grad_ref, weight_grad_hbm, store_sem.at[1])
    store_wg.start()

    await_group(ret_send, ret_sems.at[0], block)
    await_sent(full_send, full_recv.at[0], full_ss, full_rs)
    store_eg.wait()
    store_wg.wait()


def hand_over(a, b, c, a_out, b_out, c_out):
    a_out[...] = a[...]
    b_out[...] = b[...]
    c_out[...] = c[...]


def on_device(n_dp, n_chain, events, destinations, history_ids, cotangent, w_uvqk, w_out):
    _, rows, width = events.shape
    head = width // HEADS
    tokens = rows * n_chain
    per_peer = rows // n_dp
    fold = max(1, 16 // per_peer)
    total = rows * fold
    cols = width // fold
    share = width // n_dp
    vmem = pl.BlockSpec(memory_space=pltpu.VMEM)
    anywhere = pl.BlockSpec(memory_space=pl.ANY)
    pair = pltpu.SemaphoreType.DMA((2,))
    quad = pltpu.SemaphoreType.DMA((rows // share,))
    ring = pltpu.SemaphoreType.DMA((n_chain,))
    results = pl.pallas_call(
        functools.partial(kernel, n_dp, n_chain),
        out_shape=(
            jax.ShapeDtypeStruct((rows, width), BF),
            jax.ShapeDtypeStruct((rows, width), BF),
            jax.ShapeDtypeStruct((share, width), F32),
        ),
        in_specs=[anywhere, anywhere, anywhere, anywhere, anywhere, anywhere],
        out_specs=(anywhere, anywhere, anywhere),
        scratch_shapes=[
            pltpu.VMEM((1, rows), I32),
            pltpu.VMEM((1, tokens), I32),
            pltpu.VMEM((rows, width), BF),
            pltpu.VMEM((width, width), BF),
            pltpu.VMEM((rows, width), BF),
            pltpu.VMEM((rows, width), BF),
            pltpu.VMEM((share, width), F32),
            pltpu.VMEM((width, 4 * width), BF),
            pltpu.VMEM((width, width), BF),
            pltpu.VMEM((total, cols + rows), BF),
            pltpu.VMEM((total, cols + rows), BF),
            pltpu.VMEM((rows, width), F32),
            pltpu.VMEM((rows, width), BF),
            pltpu.VMEM((rows, 4 * width), F32),
            pltpu.VMEM((rows, width), BF),
            pltpu.VMEM((rows, width), F32),
            pltpu.VMEM((n_chain, rows, 3 * head), BF),
            pltpu.VMEM((tokens, 3 * head), BF),
            pltpu.VMEM((tokens, rows), F32),
            pltpu.VMEM((tokens, tokens), BF),
            pltpu.VMEM((tokens, tokens), F32),
            pltpu.VMEM((tokens, tokens), BF),
            pltpu.VMEM((tokens, head), BF),
            pltpu.VMEM((n_chain, rows, head), BF),
            pltpu.VMEM((n_chain, rows, head), BF),
            pltpu.VMEM((tokens, head), BF),
            pltpu.VMEM((8, tokens // 2), F32),
            pltpu.VMEM((n_chain, 8, tokens // 2), F32),
            pltpu.VMEM((head, tokens), F32),
            pltpu.VMEM((head, tokens), BF),
            pltpu.VMEM((head, tokens), BF),
            pltpu.VMEM((head, tokens), BF),
            pltpu.VMEM((tokens, head), BF),
            pltpu.VMEM((rows, width), BF),
            pltpu.VMEM((width // rows, rows, rows), BF),
            pltpu.VMEM((width, rows), BF),
            pltpu.VMEM((rows // share, share, width), BF),
            pltpu.VMEM((rows // share, share, width), BF),
            pltpu.VMEM((n_chain, rows, 3 * head), BF),
            pltpu.VMEM((n_chain, rows, 3 * head), BF),
            pltpu.VMEM((rows, 4 * width), BF),
            pltpu.VMEM((rows, width), F32),
            pltpu.VMEM((n_chain, share, head), BF),
            pltpu.VMEM((n_chain, share, head), BF),
            pltpu.VMEM((share, head), BF),
            pltpu.VMEM((n_chain, share, head), BF),
            pltpu.VMEM((total, total), BF),
            pltpu.VMEM((fold, rows, total), BF),
            pltpu.VMEM((rows, rows), F32),
            pltpu.VMEM((total, cols), BF),
            pltpu.VMEM((total, cols), BF),
            pltpu.SemaphoreType.DMA((6,)),
            pltpu.SemaphoreType.DMA((3,)),
            pair,
            pair,
            pair,
            quad,
            quad,
            pair,
        ]
        + [ring] * 14,
        compiler_params=pltpu.CompilerParams(
            collective_id=0, has_side_effects=True, vmem_limit_bytes=56 * 1024 * 1024
        ),
        cost_estimate=pl.CostEstimate(
            flops=9 * 2**30, bytes_accessed=12 * 2**20, transcendentals=4 * 2**20
        ),
        name="hstu_layer",
    )(destinations, history_ids, events[0], cotangent[0], w_uvqk, w_out)
    event_grad, layer_out, weight_grad = pl.pallas_call(
        hand_over,
        out_shape=tuple(jax.ShapeDtypeStruct(r.shape, r.dtype) for r in results),
        in_specs=[vmem] * 3,
        out_specs=(vmem,) * 3,
        name="hand_over",
    )(*results)
    return (layer_out[None], event_grad[None], weight_grad)


def solution(mesh):
    return jax.shard_map(
        functools.partial(on_device, mesh.shape["dp"], mesh.shape["chain"]),
        mesh=mesh,
        in_specs=(
            P("dp", "chain", None),
            P("dp", "chain"),
            P("dp", None),
            P("dp", "chain", None),
            P(),
            P(),
        ),
        out_specs=(P("dp", "chain", None), P("dp", "chain", None), P("dp", None)),
        check_vma=False,
    )
```

```python
import functools
import math

import jax
import jax.numpy as jnp
from jax import lax
from jax.experimental import pallas as pl
from jax.experimental.pallas import tpu as pltpu
from jax.sharding import PartitionSpec as P

HEADS = 8
MESH = pl.DeviceIdType.MESH
BF = jnp.bfloat16
F32 = jnp.float32
I32 = jnp.int32
epsilon = 1e-05


def dot(a, b):
    return lax.dot_general(a, b, (((1,), (0,)), ((), ())), preferred_element_type=F32)


def dot_nt(a, b):
    return lax.dot_general(a, b, (((1,), (1,)), ((), ())), preferred_element_type=F32)


def dot_tn(a, b):
    return lax.dot_general(a, b, (((0,), (0,)), ((), ())), preferred_element_type=F32)


def sigmoid(v):
    return 0.5 * jnp.tanh(0.5 * v) + 0.5


def iota(shape, dim):
    return lax.broadcasted_iota(I32, shape, dim)


def mean(v):
    return jnp.mean(v, axis=-1, keepdims=True)


def one_hot(mask):
    return jnp.where(mask, 1.0, 0.0).astype(BF)


def kernel(
    n_dp,
    n_chain,
    dest_hbm,
    hist_hbm,
    ev_hbm,
    ct_hbm,
    wu_hbm,
    wo_hbm,
    event_grad_hbm,
    layer_out_hbm,
    weight_grad_hbm,
    dest_ref,
    hist_ref,
    ev_ref,
    ct_all,
    event_grad_ref,
    layer_out_ref,
    weight_grad_ref,
    wu,
    wo,
    ev_send,
    ev_recv,
    residual_ref,
    normed_ref,
    pre_ref,
    gating_ref,
    gated_grad_ref,
    qkv_send,
    qkv,
    hist_col,
    att,
    slope,
    sgrad,
    mix_send,
    mix_recv,
    h_send,
    h_recv,
    stat_send,
    stat_recv,
    mix_t,
    key_t,
    value_t,
    mg_t,
    mg,
    gated_ref,
    gt_send,
    gt_recv,
    wg_send,
    wg_recv,
    d_send,
    d_recv,
    pg_ref,
    ng_ref,
    part_send,
    part_recv,
    full_send,
    full_recv,
    back_ref,
    home_ref,
    inverse_ref,
    ret_send,
    ret_recv,
    load_sem,
    store_sem,
    ev_sems,
    ct_sems,
    gt_sems,
    wg_ss,
    wg_rs,
    ret_sems,
    qkv_ss,
    qkv_rs,
    mix_ss,
    mix_rs,
    h_ss,
    h_rs,
    stat_ss,
    stat_rs,
    d_ss,
    d_rs,
    part_ss,
    part_rs,
    full_ss,
    full_rs,
):
    rows, width = ev_ref.shape
    head = width // HEADS
    tokens = rows * n_chain
    per_peer = rows // n_dp
    fold = max(1, 16 // per_peer)
    block = per_peer * fold
    total = rows * fold
    cols = width // fold
    alpha = head ** (-0.5)
    share = width // n_dp
    e = lax.axis_index("dp")
    c = lax.axis_index("chain")
    team = width // rows
    teams = n_dp // team
    seat = lax.rem(e, team)
    ct_ref = ct_all.at[pl.ds(pl.multiple_of(seat * rows, rows), rows)]

    load_ev = pltpu.make_async_copy(ev_hbm, ev_ref, load_sem.at[2])
    load_ct = pltpu.make_async_copy(ct_hbm, ct_ref, load_sem.at[3])
    load_wu = pltpu.make_async_copy(wu_hbm, wu, load_sem.at[0])
    load_wo = pltpu.make_async_copy(wo_hbm, wo, load_sem.at[1])
    load_dest = pltpu.make_async_copy(dest_hbm, dest_ref, load_sem.at[4])
    load_hist = pltpu.make_async_copy(hist_hbm, hist_ref, load_sem.at[5])
    load_dest.start()
    load_ev.start()
    load_hist.start()

    barrier = pltpu.get_barrier_semaphore()

    def greet(step, carry):
        pl.semaphore_signal(
            barrier, inc=1, device_id=(lax.rem(e + step, n_dp), c), device_id_type=MESH
        )
        return carry

    lax.fori_loop(1, n_dp, greet, 0)
    for step in range(1, n_chain):
        pl.semaphore_signal(
            barrier, inc=1, device_id=(e, lax.rem(c + step, n_chain)), device_id_type=MESH
        )

    load_wu.start()
    load_ct.start()
    load_wo.start()

    ri = iota((rows, rows), 0)
    ci = iota((rows, rows), 1)
    eye = ri == ci
    load_dest.wait()
    d_row = jnp.broadcast_to(dest_ref[...], (rows, rows))
    d_col = jnp.sum(jnp.where(eye, d_row.astype(F32), 0.0), axis=1, keepdims=True)
    d_col = jnp.broadcast_to(d_col, (rows, rows)).astype(I32)
    t_row = d_row // rows
    t_col = d_col // rows
    same = t_row == t_col
    rank_row = jnp.sum(jnp.where(same & (ri < ci), 1.0, 0.0), axis=0, keepdims=True)
    rank_col = jnp.sum(jnp.where(same & (ci < ri), 1.0, 0.0), axis=1, keepdims=True)
    place_row = block * t_row[:1, :] + rank_row.astype(I32)
    place_col = block * t_col + jnp.broadcast_to(rank_col, (rows, rows)).astype(I32)
    slots = (d_col - t_col * rows).astype(F32).astype(BF)
    at_row = jnp.broadcast_to(place_row, (total, rows))
    at = iota((total, rows), 0)
    spread = jnp.concatenate(
        [one_hot(at == at_row + per_peer * q) for q in range(fold)], axis=1
    )
    load_ev.wait()
    packed = jnp.concatenate(
        [
            jnp.concatenate([ev_ref[:, cols * q : cols * (q + 1)], slots], axis=1)
            for q in range(fold)
        ],
        axis=0,
    )
    ev_send[...] = dot(spread, packed).astype(BF)
    own_ev = pl.ds(pl.multiple_of(e * block, block), block)
    ev_recv[own_ev, :] = ev_send[own_ev, :]

    pl.semaphore_wait(barrier, n_dp - 1 + n_chain - 1)

    def to_group(send, recv, sems, rows_each):
        here = pl.ds(pl.multiple_of(e * rows_each, rows_each), rows_each)

        def one(step, carry):
            peer = lax.rem(e + step, n_dp)
            there = pl.ds(pl.multiple_of(peer * rows_each, rows_each), rows_each)
            pltpu.make_async_remote_copy(
                src_ref=send.at[there],
                dst_ref=recv.at[here],
                send_sem=sems.at[0],
                recv_sem=sems.at[1],
                device_id=(peer, c),
                device_id_type=MESH,
            ).start()
            return carry

        return one

    def await_group(buffer, sem, rows_each, peers=n_dp - 1):
        part = buffer.at[pl.ds(0, peers * rows_each)]
        pltpu.make_async_copy(part, part, sem).wait()

    lax.fori_loop(1, n_dp, to_group(ev_send, ev_recv, ev_sems, block), 0)

    load_hist.wait()
    for b in range(n_chain):
        ids = jnp.broadcast_to(
            hist_ref[:, rows * b : rows * (b + 1)].astype(F32), (rows, rows)
        )
        hist_col[rows * b : rows * (b + 1), :] = jnp.broadcast_to(
            jnp.sum(jnp.where(eye, ids, 0.0), axis=1, keepdims=True), (rows, rows)
        )

    def to_team(src, dst, sems):
        for step in range(1, team):
            other = lax.rem(seat + step, team)
            pltpu.make_async_remote_copy(
                src_ref=src(other),
                dst_ref=dst,
                send_sem=sems.at[0],
                recv_sem=sems.at[1],
                device_id=(e - seat + other, c),
                device_id_type=MESH,
            ).start()

    await_group(ev_recv, ev_sems.at[1], block)
    load_ct.wait()
    slot_col = ev_recv[:, cols : cols + rows].astype(F32).astype(I32)
    slot_row = jnp.concatenate(
        [
            jnp.sum(
                jnp.where(eye, slot_col[rows * b : rows * (b + 1), :], 0).astype(F32),
                axis=0,
                keepdims=True,
            )
            for b in range(fold)
        ],
        axis=1,
    ).astype(I32)
    slot_row = jnp.broadcast_to(slot_row, (rows, total))
    slot_here = slot_row == iota((rows, total), 0)
    quarter = lax.rem(iota((rows, total), 1), block) // per_peer
    arrived = ev_recv[:, :cols]
    residual = jnp.concatenate(
        [dot(one_hot(slot_here & (quarter == q)), arrived) for q in range(fold)], axis=1
    )
    residual_ref[...] = residual
    center = residual - mean(residual)
    inverse = lax.rsqrt(mean(center * center) + epsilon)
    normed_ref[...] = (center * inverse).astype(BF)

    def chain_copy(src, dst, send_sem, recv_sem, peer):
        away = lax.rem(peer - c + n_chain, n_chain)
        return pltpu.make_async_remote_copy(
            src_ref=src,
            dst_ref=dst,
            send_sem=send_sem.at[away],
            recv_sem=recv_sem.at[away],
            device_id=(e, peer),
            device_id_type=MESH,
        )

    mine = pl.ds(pl.multiple_of(c * rows, rows), rows)

    load_wu.wait()
    for turn in (2, 1, 3, 0):
        pair = lax.rem(c // 2 + turn, n_chain // 2)
        for slot, part in ((0, 2), (1, 3), (2, 1)):
            columns = pl.ds(pl.multiple_of(part * width + pair * 2 * head, 2 * head), 2 * head)
            pre = dot(normed_ref[...], wu[:, columns])
            pre_ref[:, columns] = pre
            act = (pre * sigmoid(pre)).astype(BF)
            for b in range(2):
                qkv_send[2 * pair + b, :, slot * head : (slot + 1) * head] = act[
                    :, b * head : (b + 1) * head
                ]
        for b in range(2):
            peer = 2 * pair + b

            @pl.when(peer != c)
            def _(peer=peer):
                chain_copy(qkv_send.at[peer], qkv.at[mine], qkv_ss, qkv_rs, peer).start()

    qkv[mine, :] = qkv_send[c]

    pre = dot(normed_ref[...], wu[:, :width])
    sig = sigmoid(pre)
    gating_ref[...] = (pre * sig).astype(BF)
    pre_ref[:, :width] = sig * (1.0 + pre * (1.0 - sig))
    load_wo.wait()
    gated_grad = dot_nt(ct_ref[...], wo[...])
    gated_grad_ref[...] = gated_grad
    upstream = gated_grad * gating_ref[...].astype(F32)
    upstream = upstream - mean(upstream)
    for h in range(HEADS):
        h_send[h] = upstream[:, h * head : (h + 1) * head].T.astype(BF)
    for away in (4, 3, 5, 2, 6, 1, 7):
        peer = lax.rem(c + away, n_chain)
        chain_copy(h_send.at[peer], h_recv.at[c], h_ss, h_rs, peer).start()
    h_recv[c] = h_send[c]
    to_team(lambda other: ct_ref, ct_ref, ct_sems)

    def to_slope(step, carry):
        columns = pl.ds(pl.multiple_of(width + step * 512, 512), 512)
        v = pre_ref[:, columns]
        s = sigmoid(v)
        pre_ref[:, columns] = s * (1.0 + v * (1.0 - s))
        return carry

    lax.fori_loop(0, 3 * width // 512, to_slope, 0)

    def await_one(src, dst, send_sem, recv_sem, away):
        pltpu.make_async_remote_copy(
            src_ref=src,
            dst_ref=dst,
            send_sem=send_sem.at[away],
            recv_sem=recv_sem.at[away],
            device_id=(e, c),
            device_id_type=MESH,
        ).wait_recv()

    def await_chain(src, dst, send_sem, recv_sem):
        for away in range(1, n_chain):
            await_one(src, dst, send_sem, recv_sem, away)

    def await_sent(src, dst, send_sem, recv_sem):
        for away in range(1, n_chain):
            pltpu.make_async_remote_copy(
                src_ref=src,
                dst_ref=dst,
                send_sem=send_sem.at[away],
                recv_sem=recv_sem.at[away],
                device_id=(e, c),
                device_id_type=MESH,
            ).wait_send()

    await_chain(qkv_send.at[0], qkv.at[pl.ds(0, rows)], qkv_ss, qkv_rs)

    tile = 2 * rows
    tiles = tokens // tile
    key_t[...] = qkv[:, head : 2 * head].T
    value_t[...] = qkv[:, 2 * head :].T
    upper = iota((tile, tile), 0) <= iota((tile, tile), 1)
    for i in range(tiles):
        at_i = slice(tile * i, tile * (i + 1))
        until = slice(0, tile * (i + 1))
        query_ids = hist_ref[:, at_i].astype(F32)
        for j in range(i + 1):
            at_j = slice(tile * j, tile * (j + 1))
            scores = dot_nt(qkv[at_j, head : 2 * head], qkv[at_i, :head]) * alpha
            ids = hist_col[at_j, :]
            visible = jnp.concatenate([ids, ids], axis=1) == query_ids
            if i == j:
                visible = visible & upper
            sig = sigmoid(scores)
            att[at_j, at_i] = jnp.where(visible, scores * sig, 0.0).astype(BF)
            slope[at_j, at_i] = jnp.where(
                visible, (alpha * sig) * (1.0 + scores * (1.0 - sig)), 0.0
            )
        mix_t[:, at_i] = dot(value_t[:, until], att[until, at_i])

    await_chain(h_send.at[0], h_recv.at[0], h_ss, h_rs)
    mixed = mix_t[...]
    upstream = jnp.concatenate([h_recv[k] for k in range(n_chain)], axis=1).astype(F32)
    own_mean = jnp.mean(mixed, axis=0, keepdims=True)
    center = mixed - own_mean
    half = tokens // 2
    stats = jnp.zeros((8, half), F32)
    line_no = iota((8, half), 0)
    for k, stat in enumerate(
        (
            own_mean,
            jnp.sum(center * center, axis=0, keepdims=True),
            jnp.sum(upstream, axis=0, keepdims=True),
            jnp.sum(upstream * center, axis=0, keepdims=True),
        )
    ):
        stats = jnp.where(line_no == k, stat[:, :half], stats)
        stats = jnp.where(line_no == 4 + k, stat[:, half:], stats)
    stat_send[...] = stats
    for away in (4, 3, 5, 2, 6, 1, 7):
        peer = lax.rem(c + away, n_chain)
        chain_copy(stat_send, stat_recv.at[c], stat_ss, stat_rs, peer).start()
    stat_recv[c] = stats

    for i in range(tiles):
        at_i = slice(tile * i, tile * (i + 1))
        mix_send[at_i, :] = mix_t[:, at_i].T.astype(BF)
    for away in (4, 3, 5, 2, 6, 1, 7):
        peer = lax.rem(c + away, n_chain)
        there = pl.ds(pl.multiple_of(peer * rows, rows), rows)
        chain_copy(mix_send.at[there], mix_recv.at[c], mix_ss, mix_rs, peer).start()
    mix_recv[c] = mix_send[mine, :]

    await_chain(stat_send, stat_recv.at[0], stat_ss, stat_rs)
    halves = []
    for k in range(2):
        means, squares, sums, products = (
            [stat_recv[h, 4 * k + n : 4 * k + n + 1, :] for h in range(HEADS)] for n in range(4)
        )
        middle = sum(means) / HEADS
        squares = sum(squares) + head * sum((m - middle) * (m - middle) for m in means)
        products = sum(products) + sum(u * (m - middle) for u, m in zip(sums, means))
        inverse = lax.rsqrt(squares / width + epsilon)
        tilt = inverse * inverse * inverse * (products / width)
        halves.append((middle, inverse, sum(sums) / width, tilt))
    middle, inverse, lift, tilt = (
        jnp.concatenate([halves[0][n], halves[1][n]], axis=1) for n in range(4)
    )
    mixed_grad = inverse * (upstream - lift) - tilt * (mix_t[...] - middle)
    mg_t[...] = mixed_grad.astype(BF)
    mg[...] = mixed_grad.T.astype(BF)

    for i in range(tiles - 1, -1, -1):
        at_i = slice(tile * i, tile * (i + 1))
        until = slice(0, tile * (i + 1))
        after = slice(tile * i, tokens)
        for j in range(i + 1):
            at_j = slice(tile * j, tile * (j + 1))
            grad = dot(qkv[at_j, 2 * head :], mg_t[:, at_i])
            sgrad[at_j, at_i] = (grad * slope[at_j, at_i]).astype(BF)
        query_grad = dot(key_t[:, until], sgrad[until, at_i]).T
        key_grad = dot(sgrad[at_i, after], qkv[after, :head])
        value_grad = dot(att[at_i, after], mg[after, :])
        grads = jnp.concatenate([query_grad, key_grad, value_grad], axis=1).astype(BF)
        for b in range(2):
            peer = 2 * i + b
            d_send[peer] = grads[rows * b : rows * (b + 1), :]

    def send_grads(*distances):
        for away in distances:
            peer = lax.rem(c + away, n_chain)
            chain_copy(d_send.at[peer], d_recv.at[c], d_ss, d_rs, peer).start()

    send_grads(1, 7, 2, 6)
    d_recv[c] = d_send[c]

    await_chain(mix_send.at[pl.ds(0, rows)], mix_recv.at[0], mix_ss, mix_rs)
    mixed = jnp.concatenate([mix_recv[h] for h in range(HEADS)], axis=1).astype(F32)
    center = mixed - mean(mixed)
    mixed_norm = center * lax.rsqrt(mean(center * center) + epsilon)
    gating = gating_ref[...].astype(F32)
    gated_grad = gated_grad_ref[...]
    gated_ref[...] = (mixed_norm * gating).astype(BF)
    pg_ref[:, :width] = (gated_grad * mixed_norm * pre_ref[:, :width]).astype(BF)

    for h in range(team):
        gt_send[h] = gated_ref[:, h * rows : (h + 1) * rows]
    own_gt = pl.ds(pl.multiple_of(seat * rows, rows), rows)
    to_team(lambda other: gt_send.at[other], gt_recv.at[own_gt], gt_sems)
    gt_recv[own_gt, :] = gt_send[seat]
    send_grads(3, 5)

    layer_out_ref[...] = (residual_ref[...] + dot(gated_ref[...], wo[...])).astype(BF)
    store_lo = pltpu.make_async_copy(layer_out_ref, layer_out_hbm, store_sem.at[0])
    store_lo.start()
    ng_ref[...] = dot_nt(pg_ref[:, :width], wu[:, :width])

    await_group(ct_all, ct_sems.at[1], rows, team - 1)
    await_group(gt_recv, gt_sems.at[1], rows, team - 1)
    grad_scale = 1.0 / math.sqrt(rows * n_dp * n_chain)
    term = (dot_tn(gt_recv[...], ct_all[...]) * grad_scale).astype(BF)
    line = e // team

    def wg_copy(k, owner):
        return pltpu.make_async_remote_copy(
            src_ref=wg_send.at[k],
            dst_ref=wg_recv.at[line],
            send_sem=wg_ss.at[k],
            recv_sem=wg_rs.at[line],
            device_id=(owner, c),
            device_id_type=MESH,
        )

    for k in range(teams):
        wg_send[k] = term[k * share : (k + 1) * share, :]
        owner = seat * teams + k

        @pl.when(owner != e)
        def _(k=k, owner=owner):
            wg_copy(k, owner).start()

        @pl.when(owner == e)
        def _(k=k):
            wg_recv[line] = wg_send[k]

    send_grads(4)

    summed = None
    for k in range(teams):
        @pl.when(k * team + e // teams != e)
        def _(k=k):
            pltpu.make_async_copy(wg_recv.at[k], wg_recv.at[k], wg_rs.at[k]).wait()

    for k in range(teams):
        part = wg_recv[k].astype(F32)
        summed = part if summed is None else summed + part
    summed = summed.astype(BF)
    for h in range(n_chain):
        part_send[h] = summed[:, h * head : (h + 1) * head]
    for away in (4, 3, 5, 2, 6, 1, 7):
        peer = lax.rem(c + away, n_chain)
        chain_copy(part_send.at[peer], part_recv.at[c], part_ss, part_rs, peer).start()
    part_recv[c] = part_send[c]

    residual = residual_ref[...]
    center = residual - mean(residual)
    inverse = lax.rsqrt(mean(center * center) + epsilon)
    residual_ref[...] = center * inverse
    inverse_ref[...] = jnp.broadcast_to(inverse, (rows, rows))
    slot_col = ev_recv[:, cols : cols + rows].astype(F32).astype(I32)
    slot_there = slot_col == iota((total, rows), 1)
    quarter = lax.rem(iota((total, rows), 0), block) // per_peer
    for q in range(fold):
        back_ref[:, q * rows : (q + 1) * rows] = one_hot(slot_there & (quarter == q))
    place = jnp.concatenate([place_col] * fold, axis=1)
    here = iota((rows, total), 1)
    for q in range(fold):
        home_ref[q] = one_hot(here == place + per_peer * q)

    for pair in ((0, 1), (7, 2), (6, 3), (5, 4)):
        for away in pair:
            if away:
                await_one(d_send.at[0], d_recv.at[0], d_ss, d_rs, away)
        froms = [lax.rem(c - away + n_chain, n_chain) for away in pair]
        terms = []
        for slot, part in ((0, 2), (1, 3), (2, 1)):
            spans = [
                pl.ds(pl.multiple_of(part * width + h * head, head), head) for h in froms
            ]
            grads = [
                (
                    d_recv[h, :, slot * head : (slot + 1) * head].astype(F32)
                    * pre_ref[:, span]
                ).astype(BF)
                for h, span in zip(froms, spans)
            ]
            terms.append(
                dot_nt(
                    jnp.concatenate(grads, axis=1),
                    jnp.concatenate([wu[:, span] for span in spans], axis=1),
                )
            )
        ng_ref[...] += terms[0] + terms[1] + terms[2]
    normed_grad = ng_ref[...]
    normed = residual_ref[...]
    input_grad = ct_ref[...].astype(F32) + inverse_ref[:, :1] * (
        normed_grad - mean(normed_grad) - normed * mean(normed_grad * normed)
    )
    input_grad = input_grad.astype(BF)

    stacked = jnp.concatenate(
        [input_grad[:, cols * q : cols * (q + 1)] for q in range(fold)], axis=0
    )
    ret_send[...] = dot(back_ref[...], stacked).astype(BF)
    ret_recv[own_ev, :] = ret_send[own_ev, :]
    lax.fori_loop(1, n_dp, to_group(ret_send, ret_recv, ret_sems, block), 0)

    await_chain(part_send.at[0], part_recv.at[0], part_ss, part_rs)
    whole = part_recv[0].astype(F32)
    for h in range(1, n_chain):
        whole = whole + part_recv[h].astype(F32)
    full_send[...] = whole.astype(BF)
    for away in (4, 3, 5, 2, 6, 1, 7):
        peer = lax.rem(c + away, n_chain)
        chain_copy(full_send, full_recv.at[c], full_ss, full_rs, peer).start()
    full_recv[c] = full_send[...]

    await_group(ev_send, ev_sems.at[0], block)
    await_group(ct_all, ct_sems.at[0], rows, team - 1)
    await_group(gt_recv, gt_sems.at[0], rows, team - 1)
    for k in range(teams):
        @pl.when(seat * teams + k != e)
        def _(k=k):
            pltpu.make_async_copy(wg_send.at[k], wg_send.at[k], wg_ss.at[k]).wait()

    await_sent(qkv_send.at[0], qkv.at[pl.ds(0, rows)], qkv_ss, qkv_rs)
    await_sent(mix_send.at[pl.ds(0, rows)], mix_recv.at[0], mix_ss, mix_rs)
    await_sent(h_send.at[0], h_recv.at[0], h_ss, h_rs)
    await_sent(stat_send, stat_recv.at[0], stat_ss, stat_rs)
    await_sent(d_send.at[0], d_recv.at[0], d_ss, d_rs)
    await_sent(part_send.at[0], part_recv.at[0], part_ss, part_rs)
    store_lo.wait()

    await_group(ret_recv, ret_sems.at[1], block)
    returned = ret_recv[...]
    for q in range(fold):
        event_grad_ref[:, cols * q : cols * (q + 1)] = dot(home_ref[q], returned).astype(BF)
    store_eg = pltpu.make_async_copy(event_grad_ref, event_grad_hbm, store_sem.at[2])
    store_eg.start()

    await_chain(full_send, full_recv.at[0], full_ss, full_rs)
    for h in range(n_chain):
        weight_grad_ref[:, h * head : (h + 1) * head] = full_recv[h].astype(F32)
    store_wg = pltpu.make_async_copy(weight_grad_ref, weight_grad_hbm, store_sem.at[1])
    store_wg.start()

    await_group(ret_send, ret_sems.at[0], block)
    await_sent(full_send, full_recv.at[0], full_ss, full_rs)
    store_eg.wait()
    store_wg.wait()


def hand_over(a, b, c, a_out, b_out, c_out):
    a_out[...] = a[...]
    b_out[...] = b[...]
    c_out[...] = c[...]


def on_device(n_dp, n_chain, events, destinations, history_ids, cotangent, w_uvqk, w_out):
    _, rows, width = events.shape
    head = width // HEADS
    tokens = rows * n_chain
    per_peer = rows // n_dp
    fold = max(1, 16 // per_peer)
    total = rows * fold
    cols = width // fold
    share = width // n_dp
    vmem = pl.BlockSpec(memory_space=pltpu.VMEM)
    anywhere = pl.BlockSpec(memory_space=pl.ANY)
    pair = pltpu.SemaphoreType.DMA((2,))
    quad = pltpu.SemaphoreType.DMA((rows // share,))
    ring = pltpu.SemaphoreType.DMA((n_chain,))
    results = pl.pallas_call(
        functools.partial(kernel, n_dp, n_chain),
        out_shape=(
            jax.ShapeDtypeStruct((rows, width), BF),
            jax.ShapeDtypeStruct((rows, width), BF),
            jax.ShapeDtypeStruct((share, width), F32),
        ),
        in_specs=[anywhere, anywhere, anywhere, anywhere, anywhere, anywhere],
        out_specs=(anywhere, anywhere, anywhere),
        scratch_shapes=[
            pltpu.VMEM((1, rows), I32),
            pltpu.VMEM((1, tokens), I32),
            pltpu.VMEM((rows, width), BF),
            pltpu.VMEM((width, width), BF),
            pltpu.VMEM((rows, width), BF),
            pltpu.VMEM((rows, width), BF),
            pltpu.VMEM((share, width), F32),
            pltpu.VMEM((width, 4 * width), BF),
            pltpu.VMEM((width, width), BF),
            pltpu.VMEM((total, cols + rows), BF),
            pltpu.VMEM((total, cols + rows), BF),
            pltpu.VMEM((rows, width), F32),
            pltpu.VMEM((rows, width), BF),
            pltpu.VMEM((rows, 4 * width), F32),
            pltpu.VMEM((rows, width), BF),
            pltpu.VMEM((rows, width), F32),
            pltpu.VMEM((n_chain, rows, 3 * head), BF),
            pltpu.VMEM((tokens, 3 * head), BF),
            pltpu.VMEM((tokens, rows), F32),
            pltpu.VMEM((tokens, tokens), BF),
            pltpu.VMEM((tokens, tokens), F32),
            pltpu.VMEM((tokens, tokens), BF),
            pltpu.VMEM((tokens, head), BF),
            pltpu.VMEM((n_chain, rows, head), BF),
            pltpu.VMEM((n_chain, head, rows), BF),
            pltpu.VMEM((n_chain, head, rows), BF),
            pltpu.VMEM((8, tokens // 2), F32),
            pltpu.VMEM((n_chain, 8, tokens // 2), F32),
            pltpu.VMEM((head, tokens), F32),
            pltpu.VMEM((head, tokens), BF),
            pltpu.VMEM((head, tokens), BF),
            pltpu.VMEM((head, tokens), BF),
            pltpu.VMEM((tokens, head), BF),
            pltpu.VMEM((rows, width), BF),
            pltpu.VMEM((width // rows, rows, rows), BF),
            pltpu.VMEM((width, rows), BF),
            pltpu.VMEM((rows // share, share, width), BF),
            pltpu.VMEM((rows // share, share, width), BF),
            pltpu.VMEM((n_chain, rows, 3 * head), BF),
            pltpu.VMEM((n_chain, rows, 3 * head), BF),
            pltpu.VMEM((rows, 4 * width), BF),
            pltpu.VMEM((rows, width), F32),
            pltpu.VMEM((n_chain, share, head), BF),
            pltpu.VMEM((n_chain, share, head), BF),
            pltpu.VMEM((share, head), BF),
            pltpu.VMEM((n_chain, share, head), BF),
            pltpu.VMEM((total, total), BF),
            pltpu.VMEM((fold, rows, total), BF),
            pltpu.VMEM((rows, rows), F32),
            pltpu.VMEM((total, cols), BF),
            pltpu.VMEM((total, cols), BF),
            pltpu.SemaphoreType.DMA((6,)),
            pltpu.SemaphoreType.DMA((3,)),
            pair,
            pair,
            pair,
            quad,
            quad,
            pair,
        ]
        + [ring] * 14,
        compiler_params=pltpu.CompilerParams(
            collective_id=0, has_side_effects=True, vmem_limit_bytes=56 * 1024 * 1024
        ),
        cost_estimate=pl.CostEstimate(
            flops=9 * 2**30, bytes_accessed=12 * 2**20, transcendentals=4 * 2**20
        ),
        name="hstu_layer",
    )(destinations, history_ids, events[0], cotangent[0], w_uvqk, w_out)
    event_grad, layer_out, weight_grad = pl.pallas_call(
        hand_over,
        out_shape=tuple(jax.ShapeDtypeStruct(r.shape, r.dtype) for r in results),
        in_specs=[vmem] * 3,
        out_specs=(vmem,) * 3,
        name="hand_over",
    )(*results)
    return (layer_out[None], event_grad[None], weight_grad)


def solution(mesh):
    return jax.shard_map(
        functools.partial(on_device, mesh.shape["dp"], mesh.shape["chain"]),
        mesh=mesh,
        in_specs=(
            P("dp", "chain", None),
            P("dp", "chain"),
            P("dp", None),
            P("dp", "chain", None),
            P(),
            P(),
        ),
        out_specs=(P("dp", "chain", None), P("dp", "chain", None), P("dp", None)),
        check_vma=False,
    )
```
